256 devices in a mesh: inter: 4 (over x), intra: 64 (over z, y, core).
Axes of the slice: x: 4, y: 4, z: 8, core: 2. Of those that a mesh axis runs over, the one named last changes fastest.
Arguments:
- features: bfloat16 [2048, 4096], P(('inter', 'intra')), may hold values from -6 to 6
- preact: bfloat16 [2048, 16384], P('inter', 'intra'), may hold values from -6 to 6
- upstream: bfloat16 [2048, 16384], P('inter', 'intra'), may hold values from -16 to 16
- weight: bfloat16 [4096, 16384], P(None, 'intra'), may hold values from -0.046875 to 0.046875
- pairs: int32 [2048, 2], P('inter'), may hold values from 0 to 511
- station_weight: float32 [512], replicated, may hold values from 0.3 to 3
- counts: int32 [4], P('inter'), may hold values from 1 to 512, as said below
- error: bfloat16 [16384, 16384], P('inter', 'intra'), may hold values from -0.29882812 to 0.29882812
- basis: float32 [16384, 128], P('intra'), may hold values from -6 to 6
Outputs:
- grad_input: bfloat16 [2048, 4096], P(('inter', 'intra'))
- new_error: bfloat16 [16384, 16384], P('inter', 'intra')
- new_basis: float32 [16384, 128], P('intra')
The draws below stay inside these ranges and needn't reach their ends.
Inputs may be any that keep to these rules, and one draw needn't show every extreme that they name: `pairs`: station indices. `counts`: group g holds at most ((g + 1) * 512) // 4 valid tokens and at least half as many; the last group is full.
All inputs are finite; a program needn't handle non-finite values.
Results may differ from the reference program's by a relative error of at most 0.0052.
Values may be sent and summed in bfloat16 or wider, within the bound.
No kernel may reach another device: no remote copies, remote signals or barrier semaphores. Data moves between devices by JAX's collectives and lax.ppermute only.
A program may use at most 128 MiB of HBM per device.

```python
import math
import jax
import jax.numpy as jnp
from jax import lax

D = 4096
RANK = 128
NANT = 512
GROUP_TOK = 512
COLS = 16384
TOKENS = 2048
N_INTER = 4


def draw_counts(key, part):
    key = jax.random.fold_in(key, 11)
    group_index = jnp.arange(N_INTER, dtype=jnp.int32)
    upper_bound = (group_index + 1) * GROUP_TOK // N_INTER
    lower_bound = jnp.maximum(upper_bound // 2, 1)
    drawn_counts = jax.random.randint(key, (N_INTER,), lower_bound, upper_bound + 1, dtype=jnp.int32)
    return jnp.where(group_index == N_INTER - 1, GROUP_TOK, drawn_counts).astype(jnp.int32)


def place_ends(entries, key, least, top_value):
    longest = entries.shape.index(max(entries.shape))
    spots = []
    for shift in (0, 1):
        where = [jax.random.randint(jax.random.fold_in(key, axis), (), 0, length) for axis, length in enumerate(entries.shape)]
        where[longest] = (where[longest] + shift) % entries.shape[longest]
        spots.append(tuple(where))
    return entries.at[spots[0]].set(least).at[spots[1]].set(top_value)


def with_spikes(array, stream_key, source, target, shards_of, factor):
    def block_of(dim):
        return (jnp.arange(array.shape[dim]) // (array.shape[dim] // shards_of)).reshape((-1,) + (1,) * (array.ndim - 1 - dim))

    first = jax.random.permutation(stream_key, shards_of)[block_of(target)]
    other_side = (block_of(target) + shards_of // 2) % shards_of
    return jnp.where((block_of(source) == first) | (block_of(source) == other_side), factor * array, array)


def levels(own_key, extent, pieces, low, largest):
    factor_of, own = 1.0, jax.random.fold_in(own_key, 6)
    for dim, blocks in pieces:
        heights = jnp.exp(jax.random.uniform(jax.random.fold_in(own, dim), (blocks,), jnp.float32, low / len(pieces), largest / len(pieces)))
        factor_of = factor_of * jnp.repeat(heights, extent[dim] // blocks).reshape([-1 if axis == dim else 1 for axis in range(len(extent))])
    return factor_of


def centred(own_key, dims, scale, most, shards=(), kind=jnp.bfloat16):
    result = jax.random.normal(own_key, dims, jnp.float32) * scale
    if len(shards) > 0:
        result = levels(own_key, dims, shards, -0.22, 0.18) * result
    return jnp.clip(result, min=-most, max=most).astype(kind)


def heavy_noise(key, extent, deviation, bound, shards, heavy, kind=jnp.bfloat16):
    result = deviation * jax.random.normal(key, extent, jnp.float32)
    if shards:
        result = result * levels(key, extent, shards, -0.22, 0.18)
    return jnp.clip(with_spikes(result, jax.random.fold_in(key, 3), *heavy), -bound, bound).astype(kind)


def setup_inputs(seed: int = 0) -> dict:
    arg_keys = jax.random.split(jax.random.key(seed), 10)
    return {
        "features": centred(arg_keys[0], (TOKENS, D), 1.0, 6.0, ((0, 256),)),
        "preact": centred(arg_keys[1], (TOKENS, COLS), 1.0, 6.0, ((0, 4), (1, 64))),
        "upstream": heavy_noise(arg_keys[2], (TOKENS, COLS), 1.0, 16.0, ((0, 4), (1, 64)), (1, 0, 64, 4.0)),
        "weight": centred(arg_keys[3], (D, COLS), COLS ** -0.5, 0.046875, ((1, 64),)),
        "pairs": place_ends(jax.random.randint(arg_keys[4], (TOKENS, 2), 0, NANT), jax.random.fold_in(arg_keys[4], 1), 0, NANT - 1).astype(jnp.int32),
        "station_weight": jnp.clip(jnp.exp(jax.random.uniform(arg_keys[5], (NANT,), jnp.float32, math.log(0.3), math.log(3.0))), 0.3, 3.0),
        "counts": draw_counts(jax.random.fold_in(arg_keys[9], 71), 0),
        "error": centred(arg_keys[7], (N_INTER * D, COLS), 0.05, 0.29882812, ((0, 4), (1, 64))),
        "basis": centred(arg_keys[8], (COLS, RANK), 1.0, 6.0, ((0, 64),), jnp.float32),
    }


HIGH = lax.Precision.HIGHEST

def gelu_slope(value):
    cdf = 0.5 * (1.0 + lax.erf(value / math.sqrt(2.0)))
    return cdf + value * jnp.exp(-0.5 * value * value) / math.sqrt(2.0 * math.pi)

def reference(features, preact, upstream, weight, pairs, station_weight, counts, error, basis):
    scale = station_weight[pairs[:, 0]] * station_weight[pairs[:, 1]]
    position = jnp.arange(TOKENS, dtype=jnp.int32)
    owner = position // GROUP_TOK
    live = (position % GROUP_TOK < counts[owner]).astype(jnp.float32)
    dpre = (upstream.astype(jnp.float32) * gelu_slope(preact.astype(jnp.float32)) * (scale * live)[:, None]).astype(jnp.bfloat16)
    grad_input = lax.dot_general(dpre.astype(jnp.float32), weight.astype(jnp.float32), (((1,), (1,)), ((), ())), preferred_element_type=jnp.float32).astype(jnp.bfloat16)
    mean_count = jnp.sum(counts.astype(jnp.float32)) / N_INTER
    feat_blocks = features.reshape(N_INTER, GROUP_TOK, D)
    dpre_blocks = dpre.reshape(N_INTER, GROUP_TOK, COLS)
    err_blocks = error.reshape(N_INTER, D, COLS)

    def merged_of(index):
        raw = lax.dot_general(feat_blocks[index].astype(jnp.float32), dpre_blocks[index].astype(jnp.float32), (((0,), (0,)), ((), ())), preferred_element_type=jnp.float32)
        return raw / mean_count + err_blocks[index].astype(jnp.float32)
    merged = lax.map(merged_of, jnp.arange(N_INTER, dtype=jnp.int32))

    def add_left(total, block):
        return (total + jnp.dot(block, basis, precision=HIGH), None)
    left, _ = lax.scan(add_left, jnp.zeros((D, RANK), jnp.float32), merged)
    gram = jnp.dot(left.T, left, precision=HIGH)
    chol = jnp.linalg.cholesky(gram)
    ortho = lax.linalg.triangular_solve(chol, left, left_side=False, lower=True, transpose_a=True)

    def add_right(total, block):
        return (total + lax.dot_general(block, ortho, (((0,), (0,)), ((), ())), precision=HIGH), None)
    new_basis, _ = lax.scan(add_right, jnp.zeros((COLS, RANK), jnp.float32), merged)
    decompressed = jnp.dot(ortho, new_basis.T, precision=HIGH) / N_INTER
    new_error = (merged - decompressed[None]).astype(jnp.bfloat16).reshape(N_INTER * D, COLS)
    return (grad_input, new_error, new_basis)
```

```python
import math

import jax
import jax.numpy as jnp
from jax import lax
from jax.sharding import Mesh, PartitionSpec as P

F32 = jnp.float32
BF16 = jnp.bfloat16
PLANE = ("z", "y", "c")
ALL = ("x", "z", "y", "c")


def gelu_slope(value):
    cdf = 0.5 * (1.0 + lax.erf(value / math.sqrt(2.0)))
    return cdf + value * jnp.exp(-0.5 * value * value) / math.sqrt(2.0 * math.pi)


def split(value):
    head = lax.reduce_precision(value, 8, 7)
    return head.astype(BF16), (value - head).astype(BF16)


def mm(a, b, contract):
    return lax.dot_general(a, b, (contract, ((), ())), preferred_element_type=F32)


def mm_wide(a, wide, contract):
    head, rest = split(wide)
    out = mm(a, jnp.concatenate([head, rest], axis=1), contract)
    n = wide.shape[1]
    return out[:, :n] + out[:, n:]


def swap(value, axis, bit):
    n = lax.axis_size(axis)
    return lax.ppermute(value, axis, [(i, i ^ bit) for i in range(n)])


def lookup(station_weight, column):
    onehot = (
        column[:, None] == jnp.arange(station_weight.shape[0], dtype=jnp.int32)[None, :]
    ).astype(F32)
    return jnp.dot(onehot, station_weight, precision=lax.Precision.HIGHEST)


def halve(value, axis, bit):
    mine = (lax.axis_index(axis) // bit) % 2
    half = value.shape[0] // 2
    give = lax.dynamic_slice_in_dim(value, (1 - mine) * half, half, 0).astype(BF16)
    keep = lax.dynamic_slice_in_dim(value, mine * half, half, 0)
    return keep.astype(F32) + swap(give, axis, bit).astype(F32)


def per_device(features, preact, upstream, weight, pairs, station_weight, counts, error, basis):
    n_inter = lax.axis_size("x")
    group_rows, width = preact.shape[0], features.shape[1]
    rank = basis.shape[1]
    c = lax.axis_index("c")

    own = counts.astype(F32)
    own = own + swap(own, "x", 1)
    total = (own + swap(own, "x", 2))[0]
    inv_mean = n_inter / total

    all_features = lax.all_gather(features, PLANE, axis=0, tiled=True)
    other = swap(features, "c", 1)
    pair_features = jnp.where(
        c == 0, jnp.concatenate([features, other]), jnp.concatenate([other, features])
    )

    scale = lookup(station_weight, pairs[:, 0]) * lookup(station_weight, pairs[:, 1])
    live = (jnp.arange(group_rows, dtype=jnp.int32) < counts[0]).astype(F32)
    dpre = (
        upstream.astype(F32) * gelu_slope(preact.astype(F32)) * (scale * live)[:, None]
    ).astype(BF16)

    share = mm_wide(dpre, basis, ((1,), (0,)))
    share = share + swap(share, "c", 1)

    err_left = mm_wide(error, basis, ((1,), (0,)))
    half = width // 2
    err_give = lax.dynamic_slice_in_dim(err_left, (1 - c) * half, half, 0)
    err_keep = lax.dynamic_slice_in_dim(err_left, c * half, half, 0)
    err_half = err_keep + swap(err_give, "c", 1)

    rows = dpre.reshape(2, 2, 2, 2, 2, 2, 8, dpre.shape[1])
    rows = rows.transpose(5, 4, 2, 3, 1, 0, 6, 7).reshape(dpre.shape)
    grad = mm(rows, weight, ((1,), (1,))).astype(BF16)
    grad = halve(grad, "c", 1)
    grad = halve(grad, "y", 1)

    tokens = group_rows // 32
    share = lax.all_to_all(share, ("z", "y"), 0, 0, tiled=True)
    share = share.reshape(32, tokens, rank).sum(0) * inv_mean
    pair_half = lax.dynamic_slice_in_dim(pair_features, c * half, half, 1)
    part = err_half + mm_wide(pair_half, share, ((0,), (0,)))

    grad, part = lax.optimization_barrier((grad, part))
    grad = halve(grad, "z", 1)

    part = lax.all_to_all(part, ("x", "y"), 0, 0, tiled=True)
    part = part.reshape(16, half // 16, rank).sum(0)
    for bit in (1, 2, 4):
        part = part + swap(part, "z", bit)

    grad, part = lax.optimization_barrier((grad, part))
    grad = halve(grad, "y", 2)

    mine = lax.all_to_all(
        jnp.broadcast_to(part[None], (16,) + part.shape), ("x", "y"), 0, 0, tiled=True
    ).reshape(half, rank)
    gram = jnp.dot(mine.T, mine, precision=lax.Precision.HIGHEST)
    gram = gram + swap(gram, "c", 1)
    other = swap(mine, "c", 1)
    left = jnp.where(c == 0, jnp.concatenate([mine, other]), jnp.concatenate([other, mine]))

    grad, left = lax.optimization_barrier((grad, left))
    grad = halve(grad, "z", 2)

    raw = mm(all_features, dpre, ((0,), (0,)))
    merged = raw * inv_mean + error.astype(F32)
    right = lax.dot_general(
        merged, left, (((0,), (0,)), ((), ())), precision=lax.Precision.HIGH
    )
    right = right + swap(right, "x", 1)
    right = right + swap(right, "x", 2)

    grad = halve(grad, "z", 4).astype(BF16)

    chol = jnp.linalg.cholesky(gram)
    inverse = lax.linalg.triangular_solve(
        chol, jnp.eye(rank, dtype=F32), left_side=True, lower=True
    )
    new_basis = jnp.dot(right, inverse.T, precision=lax.Precision.HIGHEST)
    back = jnp.dot(new_basis, inverse, precision=lax.Precision.HIGHEST)
    new_error = (
        merged - jnp.dot(left, back.T, precision=lax.Precision.HIGH) / n_inter
    ).astype(BF16)
    return grad, new_error, new_basis


def solution(mesh):
    mesh = Mesh(mesh.devices.reshape(4, 8, 4, 2), ALL)
    in_specs = (
        P(ALL, None),
        P("x", PLANE),
        P("x", PLANE),
        P(None, PLANE),
        P("x", None),
        P(),
        P("x"),
        P("x", PLANE),
        P(PLANE, None),
    )
    out_specs = (P(ALL, None), P("x", PLANE), P(PLANE, None))
    return jax.shard_map(
        per_device, mesh=mesh, in_specs=in_specs, out_specs=out_specs, check_vma=False
    )
```

```python
import functools, math
import jax
import jax.numpy as jnp
from jax import lax
from jax.experimental import pallas as pl
from jax.experimental.pallas import tpu as pltpu
from jax.sharding import Mesh, PartitionSpec as P

F32 = jnp.float32
BF16 = jnp.bfloat16
HIGHEST = lax.Precision.HIGHEST
VMEM = 48 * 1024 * 1024


def gelu_slope(value):
    cdf = 0.5 * (1.0 + lax.erf(value / math.sqrt(2.0)))
    return cdf + value * jnp.exp(-0.5 * value * value) / math.sqrt(2.0 * math.pi)


def split(value):
    head = value.astype(BF16)
    return head, (value - head.astype(F32)).astype(BF16)


def mm(a, b, contract):
    return lax.dot_general(a, b, (contract, ((), ())), preferred_element_type=F32)


def mm_wide(a, wide, contract):
    head, rest = split(wide)
    out = mm(a, jnp.concatenate([head, rest], axis=1), contract)
    n = wide.shape[1]
    return out[:, :n] + out[:, n:]


def mm_split(a, b, contract):
    return mm(a[0], b[0], contract) + (mm(a[0], b[1], contract) + mm(a[1], b[0], contract))


def params(**kw):
    return pltpu.CompilerParams(vmem_limit_bytes=VMEM, **kw)


def token_kernel(count_ref, pairs_ref, table_ref, up_ref, pre_ref, basis_ref, dpre_ref, share_ref):
    rows = up_ref.shape[0]
    stations = table_ref.shape[1]
    table = table_ref[...]
    head = table.astype(BF16)
    middle = (table - head.astype(F32)).astype(BF16)
    last = (table - head.astype(F32) - middle.astype(F32)).astype(BF16)
    which = lax.broadcasted_iota(jnp.int32, (stations, rows), 0)
    weight = None
    for end in range(2):
        onehot = (which == pairs_ref[end : end + 1, :]).astype(F32).astype(BF16)
        found = None
        for piece in (last, middle, head):
            term = mm(jnp.broadcast_to(piece, (16, stations)), onehot, ((1,), (0,)))[:1]
            found = term if found is None else found + term
        weight = found if weight is None else weight * found
    live = lax.broadcasted_iota(jnp.int32, (1, rows), 1) < count_ref[0]
    weight = jnp.where(live, weight, 0.0)
    column = jnp.transpose(jnp.broadcast_to(weight, (128, rows)))
    column = jnp.concatenate([column] * (up_ref.shape[1] // 128), axis=1)
    dpre = (up_ref[...].astype(F32) * gelu_slope(pre_ref[...].astype(F32)) * column).astype(BF16)
    dpre_ref[...] = dpre
    share_ref[...] = mm_wide(dpre, basis_ref[...], ((1,), (0,)))


def token_part(counts, pairs, table, upstream, preact, basis):
    vm = pl.BlockSpec(memory_space=pltpu.VMEM)
    return pl.pallas_call(
        token_kernel,
        out_shape=(
            jax.ShapeDtypeStruct(upstream.shape, BF16),
            jax.ShapeDtypeStruct((upstream.shape[0], basis.shape[1]), F32),
        ),
        in_specs=[pl.BlockSpec(memory_space=pltpu.SMEM)] + [vm] * 5,
        out_specs=(vm, vm),
        compiler_params=params(),
        cost_estimate=pl.CostEstimate(flops=10**8, bytes_accessed=10**6, transcendentals=10**5),
    )(counts, pairs.T, table[None], upstream, preact, basis)


def err_kernel(core_ref, error_ref, basis_ref, out_ref):
    out_ref[0] = mm_wide(error_ref[...], basis_ref[...], ((1,), (0,)))


def error_part(core, error, basis, step=2048):
    rows, cols = error.shape
    rank = basis.shape[1]
    half = rows // 2
    per = half // step
    return pl.pallas_call(
        err_kernel,
        out_shape=jax.ShapeDtypeStruct((2, half, rank), F32),
        grid_spec=pltpu.PrefetchScalarGridSpec(
            num_scalar_prefetch=1,
            grid=(2, per),
            in_specs=[
                pl.BlockSpec((step, cols), lambda h, i, core: ((core[0] + 1 - h) % 2 * per + i, 0)),
                pl.BlockSpec((cols, rank), lambda h, i, core: (0, 0)),
            ],
            out_specs=pl.BlockSpec((1, step, rank), lambda h, i, core: (1 - h, i, 0)),
        ),
        compiler_params=params(),
        cost_estimate=pl.CostEstimate(flops=10**9, bytes_accessed=4 * 10**6, transcendentals=0),
    )(core, error, basis)


def left_kernel(core_ref, inv_ref, share_ref, feat_ref, keep_ref, got_ref, out_ref):
    blocks = share_ref.shape[0]
    total = share_ref[0]
    for i in range(1, blocks):
        total = total + share_ref[i]
    total = total * inv_ref[0]
    out_ref[...] = keep_ref[0] + got_ref[...] + mm_wide(feat_ref[...], total, ((0,), (0,)))


def left_part(core, inv_mean, share, pair_features, err_halves, got):
    blocks, tokens, rank = share.shape
    half = got.shape[0]
    step = 1024
    per = half // step
    return pl.pallas_call(
        left_kernel,
        out_shape=jax.ShapeDtypeStruct((half, rank), F32),
        grid_spec=pltpu.PrefetchScalarGridSpec(
            num_scalar_prefetch=2,
            grid=(per,),
            in_specs=[
                pl.BlockSpec((blocks, tokens, rank), lambda i, core, inv: (0, 0, 0)),
                pl.BlockSpec((tokens, step), lambda i, core, inv: (0, core[0] * per + i)),
                pl.BlockSpec((1, step, rank), lambda i, core, inv: (0, i, 0)),
                pl.BlockSpec((step, rank), lambda i, core, inv: (i, 0)),
            ],
            out_specs=pl.BlockSpec((step, rank), lambda i, core, inv: (i, 0)),
        ),
        compiler_params=params(),
        cost_estimate=pl.CostEstimate(flops=10**8, bytes_accessed=4 * 10**6, transcendentals=0),
    )(core, inv_mean, share, pair_features, err_halves, got)


def merge_kernel(inv_ref, feat_ref, dpre_ref, error_ref, merged_ref, head_ref, rest_ref):
    raw = mm(feat_ref[...], dpre_ref[...], ((0,), (0,)))
    merged = raw * inv_ref[0] + error_ref[...].astype(F32)
    merged_ref[...] = merged
    head, rest = split(jnp.transpose(merged))
    head_ref[...] = head
    rest_ref[...] = rest


def merge_part(inv_mean, features, dpre, error):
    tokens, width = features.shape
    cols = dpre.shape[1]
    step = 512
    return pl.pallas_call(
        merge_kernel,
        out_shape=(
            jax.ShapeDtypeStruct((width, cols), F32),
            jax.ShapeDtypeStruct((cols, width), BF16),
            jax.ShapeDtypeStruct((cols, width), BF16),
        ),
        grid=(width // step,),
        in_specs=[
            pl.BlockSpec(memory_space=pltpu.SMEM),
            pl.BlockSpec((tokens, step), lambda i: (0, i)),
            pl.BlockSpec((tokens, cols), lambda i: (0, 0)),
            pl.BlockSpec((step, cols), lambda i: (i, 0)),
        ],
        out_specs=(
            pl.BlockSpec((step, cols), lambda i: (i, 0)),
            pl.BlockSpec((cols, step), lambda i: (0, i)),
            pl.BlockSpec((cols, step), lambda i: (0, i)),
        ),
        compiler_params=params(),
        cost_estimate=pl.CostEstimate(flops=2 * 10**9, bytes_accessed=16 * 10**6, transcendentals=0),
    )(inv_mean, features, dpre, error)


def right_kernel(head_ref, rest_ref, left_ref, right_ref):
    lh, ll = split(left_ref[...])
    rank = lh.shape[1]
    both = mm(head_ref[...], jnp.concatenate([lh, ll], axis=1), ((1,), (0,)))
    term = both[:, :rank] + both[:, rank:] + mm(rest_ref[...], lh, ((1,), (0,)))

    @pl.when(pl.program_id(0) == 0)
    def _():
        right_ref[...] = term

    @pl.when(pl.program_id(0) > 0)
    def _():
        right_ref[...] += term


def right_part(head, rest, left, step=2048):
    cols, width = head.shape
    rank = left.shape[1]
    return pl.pallas_call(
        right_kernel,
        out_shape=jax.ShapeDtypeStruct((cols, rank), F32),
        grid=(width // step,),
        in_specs=[
            pl.BlockSpec((cols, step), lambda i: (0, i)),
            pl.BlockSpec((cols, step), lambda i: (0, i)),
            pl.BlockSpec((step, rank), lambda i: (i, 0)),
        ],
        out_specs=pl.BlockSpec((cols, rank), lambda i: (0, 0)),
        compiler_params=params(),
        cost_estimate=pl.CostEstimate(flops=10**9, bytes_accessed=6 * 10**6, transcendentals=0),
    )(head, rest, left)


def inverse_kernel(gram_ref, out_ref):
    n = gram_ref.shape[0]
    a = gram_ref[...]
    b = (
        lax.broadcasted_iota(jnp.int32, (n, n), 0) == lax.broadcasted_iota(jnp.int32, (n, n), 1)
    ).astype(F32)
    for low in range(0, n, 8):
        left = n - low
        row_index = lax.broadcasted_iota(jnp.int32, (left, n), 0)
        columns = [
            jnp.broadcast_to(a[:, low + j : low + j + 1], (left, n)) for j in range(8)
        ]
        for j in range(8):
            column = columns[j]
            pivot = column[j : j + 1, :]
            scale = lax.rsqrt(pivot)
            scale = scale * (1.5 - 0.5 * pivot * scale * scale)
            row_a, row_b = a[j : j + 1, :], b[j : j + 1, :]
            out_ref[low + j : low + j + 1, :] = row_b * scale
            factor = jnp.where(row_index > j, column * (scale * scale), 0.0)
            for i in range(j + 1, 8):
                columns[i] = columns[i] - factor * column[i : i + 1, :]
            a = a - factor * row_a
            b = b - factor * row_b
        a, b = a[8:], b[8:]


def inverse_part(gram):
    vm = pl.BlockSpec(memory_space=pltpu.VMEM)
    return pl.pallas_call(
        inverse_kernel,
        out_shape=jax.ShapeDtypeStruct(gram.shape, F32),
        in_specs=[vm],
        out_specs=vm,
        compiler_params=params(),
        cost_estimate=pl.CostEstimate(flops=10**7, bytes_accessed=10**5, transcendentals=128),
    )(gram)


def last_kernel(merged_ref, left_ref, right_ref, inverse_ref, error_ref, basis_ref, back_ref):
    @pl.when(pl.program_id(0) == 0)
    def _():
        inverse = split(inverse_ref[...])
        basis = mm_split(split(right_ref[...]), inverse, ((1,), (1,)))
        basis_ref[...] = basis
        head, rest = split(mm_split(split(basis * 0.25), inverse, ((1,), (0,))))
        back_ref[0] = head
        back_ref[1] = rest

    out = mm_split(split(left_ref[...]), (back_ref[0], back_ref[1]), ((1,), (1,)))
    error_ref[...] = (merged_ref[...] - out).astype(BF16)


def last_part(merged, left, right, inverse, step=2048):
    width, cols = merged.shape
    rank = left.shape[1]
    whole = lambda i: (0, 0)
    return pl.pallas_call(
        last_kernel,
        out_shape=(
            jax.ShapeDtypeStruct((width, cols), BF16),
            jax.ShapeDtypeStruct((cols, rank), F32),
        ),
        grid=(width // step,),
        in_specs=[
            pl.BlockSpec((step, cols), lambda i: (i, 0)),
            pl.BlockSpec((step, rank), lambda i: (i, 0)),
            pl.BlockSpec((cols, rank), whole),
            pl.BlockSpec((rank, rank), whole),
        ],
        out_specs=(
            pl.BlockSpec((step, cols), lambda i: (i, 0)),
            pl.BlockSpec((cols, rank), whole),
        ),
        scratch_shapes=[pltpu.VMEM((2, cols, rank), BF16)],
        compiler_params=params(),
        cost_estimate=pl.CostEstimate(flops=10**9, bytes_accessed=8 * 10**6, transcendentals=0),
    )(merged, left, right, inverse)


PLANE = ("z", "y", "c")
ALL = ("x", "z", "y", "c")


def swap(value, axis, bit):
    n = lax.axis_size(axis)
    return lax.ppermute(value, axis, [(i, i ^ bit) for i in range(n)])


def per_device(features, preact, upstream, weight, pairs, station_weight, counts, error, basis):
    n_inter, n_z, n_y = lax.axis_size("x"), lax.axis_size("z"), lax.axis_size("y")
    group_rows, width = preact.shape[0], features.shape[1]
    rank, half = basis.shape[1], width // 2
    c = lax.axis_index("c")
    core = c.astype(jnp.int32)[None]

    all_features = lax.all_gather(features, PLANE, axis=0, tiled=True)
    own = counts.astype(F32)
    own = own + swap(own, "x", 1)
    other = swap(features, "c", 1)
    pair_features = jnp.where(
        c == 0, jnp.concatenate([features, other]), jnp.concatenate([other, features])
    )

    dpre, share = token_part(counts, pairs, station_weight, upstream, preact, basis)
    share = share + swap(share, "c", 1)

    own, error_late, share = lax.optimization_barrier((own, error, share))
    inv_mean = n_inter / (own + swap(own, "x", 2))
    halves = error_part(core, error_late, basis)
    halves_got = swap(halves[1], "c", 1)

    tokens = group_rows // (n_z * n_y)
    share = lax.all_to_all(share, ("z", "y"), 0, 0, tiled=True).reshape(-1, tokens, rank)
    part = left_part(core, inv_mean, share, pair_features, halves, halves_got)

    dpre_late, part = lax.optimization_barrier((dpre, part))
    rows = dpre_late.reshape(n_z, n_y, 2, 8, dpre.shape[1]).transpose(2, 1, 0, 3, 4)
    rows = rows.reshape(2, group_rows // 2, dpre.shape[1])
    give = lax.dynamic_index_in_dim(rows, 1 - c, 0, keepdims=False)
    keep = lax.dynamic_index_in_dim(rows, c, 0, keepdims=False)
    got = swap(mm(give, weight, ((1,), (1,))).astype(BF16), "c", 1)
    grad = (mm(keep, weight, ((1,), (1,))) + got.astype(F32)).astype(BF16)

    part = lax.all_to_all(part, ("x", "y"), 0, 0, tiled=True)
    part = part.reshape(n_inter * n_y, -1, rank).sum(0)

    grad, part = lax.optimization_barrier((grad, part))
    grad = lax.all_to_all(grad, "y", 0, 0, tiled=True)

    for bit in (1, 2, 4):
        part = part + swap(part, "z", bit)
    grad = grad.reshape(n_y, -1, width).astype(F32).sum(0).astype(BF16)

    grad, part = lax.optimization_barrier((grad, part))
    grad = lax.all_to_all(grad, "z", 0, 0, tiled=True)
    merged, head, rest = merge_part(inv_mean, all_features, dpre, error)
    mine = lax.all_to_all(
        jnp.broadcast_to(part[None], (n_inter * n_y,) + part.shape), ("x", "y"), 0, 0, tiled=True
    ).reshape(half, rank)
    merged, mine = lax.optimization_barrier((merged, mine))
    other = swap(mine, "c", 1)
    left = jnp.where(c == 0, jnp.concatenate([mine, other]), jnp.concatenate([other, mine]))

    right = right_part(head, rest, left)
    right_got = swap(right, "x", 1)
    mine, right = lax.optimization_barrier((mine, right))
    gram = jnp.dot(mine.T, mine, precision=HIGHEST)
    gram = gram + swap(gram, "c", 1)
    right = right + right_got
    gram, right = lax.optimization_barrier((gram, right))
    right = right + swap(right, "x", 2)
    inverse = inverse_part(gram)
    new_error, new_basis = last_part(merged, left, right, inverse)
    grad = grad.reshape(n_z, -1, width).astype(F32).sum(0).astype(BF16)
    return grad, new_error, new_basis


def solution(mesh):
    mesh = Mesh(mesh.devices.reshape(4, 8, 4, 2), ALL)
    in_specs = (
        P(ALL, None),
        P("x", PLANE),
        P("x", PLANE),
        P(None, PLANE),
        P("x", None),
        P(),
        P("x"),
        P("x", PLANE),
        P(PLANE, None),
    )
    out_specs = (P(ALL, None), P("x", PLANE), P(PLANE, None))
    return jax.shard_map(
        per_device, mesh=mesh, in_specs=in_specs, out_specs=out_specs, check_vma=False
    )
```

```python
import functools, math
import jax
import jax.numpy as jnp
from jax import lax
from jax.experimental import pallas as pl
from jax.experimental.pallas import tpu as pltpu
from jax.sharding import Mesh, PartitionSpec as P

F32 = jnp.float32
BF16 = jnp.bfloat16
HIGHEST = lax.Precision.HIGHEST
VMEM = 56 * 1024 * 1024


def gelu_slope(value):
    cdf = 0.5 * (1.0 + lax.erf(value / math.sqrt(2.0)))
    return cdf + value * jnp.exp(-0.5 * value * value) / math.sqrt(2.0 * math.pi)


def split(value):
    head = value.astype(BF16)
    return head, (value - head.astype(F32)).astype(BF16)


def mm(a, b, contract):
    return lax.dot_general(a, b, (contract, ((), ())), preferred_element_type=F32)


def mm_wide(a, wide, contract):
    head, rest = split(wide)
    out = mm(a, jnp.concatenate([head, rest], axis=1), contract)
    n = wide.shape[1]
    return out[:, :n] + out[:, n:]


def mm_split(a, b, contract):
    return mm(a[0], b[0], contract) + (mm(a[0], b[1], contract) + mm(a[1], b[0], contract))


def params(limit=VMEM):
    return pltpu.CompilerParams(vmem_limit_bytes=limit)


def token_kernel(count_ref, pairs_ref, table_ref, up_ref, pre_ref, basis_ref, dpre_ref, share_ref):
    rows = up_ref.shape[0]
    stations = table_ref.shape[1]
    table = table_ref[...]
    head = table.astype(BF16)
    middle = (table - head.astype(F32)).astype(BF16)
    last = (table - head.astype(F32) - middle.astype(F32)).astype(BF16)
    which = lax.broadcasted_iota(jnp.int32, (stations, rows), 0)
    weight = None
    for end in range(2):
        onehot = (which == pairs_ref[end : end + 1, :]).astype(F32).astype(BF16)
        found = None
        for piece in (last, middle, head):
            term = mm(jnp.broadcast_to(piece, (16, stations)), onehot, ((1,), (0,)))[:1]
            found = term if found is None else found + term
        weight = found if weight is None else weight * found
    live = lax.broadcasted_iota(jnp.int32, (1, rows), 1) < count_ref[0]
    weight = jnp.where(live, weight, 0.0)
    column = jnp.transpose(jnp.broadcast_to(weight, (128, rows)))
    column = jnp.concatenate([column] * (up_ref.shape[1] // 128), axis=1)
    dpre = (up_ref[...].astype(F32) * gelu_slope(pre_ref[...].astype(F32)) * column).astype(BF16)
    dpre_ref[...] = dpre
    share_ref[...] = mm_wide(dpre, basis_ref[...], ((1,), (0,)))


def token_part(counts, pairs, table, upstream, preact, basis):
    vm = pl.BlockSpec(memory_space=pltpu.VMEM)
    return pl.pallas_call(
        token_kernel,
        out_shape=(
            jax.ShapeDtypeStruct(upstream.shape, BF16),
            jax.ShapeDtypeStruct((upstream.shape[0], basis.shape[1]), F32),
        ),
        in_specs=[pl.BlockSpec(memory_space=pltpu.SMEM)] + [vm] * 5,
        out_specs=(vm, vm),
        compiler_params=params(),
        cost_estimate=pl.CostEstimate(flops=10**5, bytes_accessed=10**4, transcendentals=0),
    )(counts, pairs.T, table[None], upstream, preact, basis)


def err_kernel(core_ref, error_ref, basis_ref, give_ref, keep_ref):
    product = mm_wide(error_ref[...], basis_ref[...], ((1,), (0,)))

    @pl.when(pl.program_id(0) == 0)
    def _():
        give_ref[...] = product

    @pl.when(pl.program_id(0) == 1)
    def _():
        keep_ref[...] = product


def error_part(core, error, basis):
    rows, cols = error.shape
    rank, half = basis.shape[1], rows // 2
    whole = lambda h, core: (0, 0)
    return pl.pallas_call(
        err_kernel,
        out_shape=(jax.ShapeDtypeStruct((half, rank), F32),) * 2,
        grid_spec=pltpu.PrefetchScalarGridSpec(
            num_scalar_prefetch=1,
            grid=(2,),
            in_specs=[
                pl.BlockSpec((half, cols), lambda h, core: ((core[0] + 1 + h) % 2, 0)),
                pl.BlockSpec((cols, rank), whole),
            ],
            out_specs=(pl.BlockSpec((half, rank), whole),) * 2,
        ),
        compiler_params=params(),
        cost_estimate=pl.CostEstimate(flops=10**5, bytes_accessed=10**4, transcendentals=0),
    )(core, error, basis)


def left_kernel(inv_ref, share_ref, feat_ref, keep_ref, got_ref, out_ref):
    share = share_ref[0]
    for i in range(1, share_ref.shape[0]):
        share = share + share_ref[i]
    out_ref[...] = (
        keep_ref[...]
        + got_ref[...]
        + mm_wide(feat_ref[...], share * inv_ref[0], ((0,), (0,)))
    )


def left_part(inv_mean, share, feats, keep, got):
    blocks, tokens, rank = share.shape
    half = got.shape[0]
    step = half // 2
    rows = pl.BlockSpec((step, rank), lambda i: (i, 0))
    return pl.pallas_call(
        left_kernel,
        out_shape=jax.ShapeDtypeStruct((half, rank), F32),
        grid=(half // step,),
        in_specs=[
            pl.BlockSpec(memory_space=pltpu.SMEM),
            pl.BlockSpec((blocks, tokens, rank), lambda i: (0, 0, 0)),
            pl.BlockSpec((tokens, step), lambda i: (0, i)),
            rows,
            rows,
        ],
        out_specs=rows,
        compiler_params=params(),
        cost_estimate=pl.CostEstimate(flops=10**8, bytes_accessed=4 * 10**6, transcendentals=0),
    )(inv_mean, share, feats, keep, got)


def merge_kernel(inv_ref, feat_ref, dpre_ref, error_ref, merged_ref, head_ref, rest_ref):
    raw = mm(feat_ref[...], dpre_ref[...], ((0,), (0,)))
    merged = raw * inv_ref[0] + error_ref[...].astype(F32)
    merged_ref[...] = merged
    head, rest = split(jnp.transpose(merged))
    head_ref[...] = head
    rest_ref[...] = rest


def merge_part(inv_mean, features, dpre, error):
    tokens, width = features.shape
    cols = dpre.shape[1]
    step = 512
    return pl.pallas_call(
        merge_kernel,
        out_shape=(
            jax.ShapeDtypeStruct((width, cols), F32),
            jax.ShapeDtypeStruct((cols, width), BF16),
            jax.ShapeDtypeStruct((cols, width), BF16),
        ),
        grid=(width // step,),
        in_specs=[
            pl.BlockSpec(memory_space=pltpu.SMEM),
            pl.BlockSpec((tokens, step), lambda i: (0, i)),
            pl.BlockSpec((tokens, cols), lambda i: (0, 0)),
            pl.BlockSpec((step, cols), lambda i: (i, 0)),
        ],
        out_specs=(
            pl.BlockSpec((step, cols), lambda i: (i, 0)),
            pl.BlockSpec((cols, step), lambda i: (0, i)),
            pl.BlockSpec((cols, step), lambda i: (0, i)),
        ),
        compiler_params=params(),
        cost_estimate=pl.CostEstimate(flops=2 * 10**9, bytes_accessed=16 * 10**6, transcendentals=0),
    )(inv_mean, features, dpre, error)


def right_kernel(core_ref, head_ref, rest_ref, own_ref, other_ref, right_ref):
    def term(left):
        lh, ll = split(left)
        rank = lh.shape[1]
        both = mm(head_ref[...], jnp.concatenate([lh, ll], axis=1), ((1,), (0,)))
        return both[:, :rank] + both[:, rank:] + mm(rest_ref[...], lh, ((1,), (0,)))

    @pl.when(pl.program_id(0) == 0)
    def _():
        right_ref[...] = term(own_ref[...])

    @pl.when(pl.program_id(0) == 1)
    def _():
        right_ref[...] += term(other_ref[...])


def right_part(core, head, rest, own, other):
    cols, width = head.shape
    half, rank = own.shape
    whole = lambda h, core: (0, 0)
    column = pl.BlockSpec((cols, half), lambda h, core: (0, (core[0] + h) % 2))
    return pl.pallas_call(
        right_kernel,
        out_shape=jax.ShapeDtypeStruct((cols, rank), F32),
        grid_spec=pltpu.PrefetchScalarGridSpec(
            num_scalar_prefetch=1,
            grid=(2,),
            in_specs=[column, column] + [pl.BlockSpec((half, rank), whole)] * 2,
            out_specs=pl.BlockSpec((cols, rank), whole),
        ),
        compiler_params=params(),
        cost_estimate=pl.CostEstimate(flops=10**9, bytes_accessed=6 * 10**6, transcendentals=0),
    )(core, head, rest, own, other)


def inverse_kernel(gram_ref, out_ref):
    n = gram_ref.shape[0]
    a = gram_ref[...]
    b = (
        lax.broadcasted_iota(jnp.int32, (n, n), 0) == lax.broadcasted_iota(jnp.int32, (n, n), 1)
    ).astype(F32)
    for low in range(0, n, 8):
        left = n - low
        row_index = lax.broadcasted_iota(jnp.int32, (left, n), 0)
        columns = [
            jnp.broadcast_to(a[:, low + j : low + j + 1], (left, n)) for j in range(8)
        ]
        for j in range(8):
            column = columns[j]
            pivot = column[j : j + 1, :]
            scale = lax.rsqrt(pivot)
            scale = scale * (1.5 - 0.5 * pivot * scale * scale)
            row_a, row_b = a[j : j + 1, :], b[j : j + 1, :]
            out_ref[low + j : low + j + 1, :] = row_b * scale
            factor = jnp.where(row_index > j, column * (scale * scale), 0.0)
            for i in range(j + 1, 8):
                columns[i] = columns[i] - factor * column[i : i + 1, :]
            a = a - factor * row_a
            b = b - factor * row_b
        a, b = a[8:], b[8:]


def inverse_part(gram):
    vm = pl.BlockSpec(memory_space=pltpu.VMEM)
    return pl.pallas_call(
        inverse_kernel,
        out_shape=jax.ShapeDtypeStruct(gram.shape, F32),
        in_specs=[vm],
        out_specs=vm,
        compiler_params=params(VMEM // 8),
        cost_estimate=pl.CostEstimate(flops=10**7, bytes_accessed=10**5, transcendentals=128),
    )(gram)


def last_kernel(core_ref, merged_ref, own_ref, other_ref, right_ref, inverse_ref, error_ref, basis_ref, back_ref):
    def fill(left):
        out = mm_split(split(left), (back_ref[0], back_ref[1]), ((1,), (1,)))
        error_ref[...] = (merged_ref[...] - out).astype(BF16)

    @pl.when(pl.program_id(0) == 0)
    def _():
        inverse = split(inverse_ref[...])
        basis = mm_split(split(right_ref[...]), inverse, ((1,), (1,)))
        basis_ref[...] = basis
        head, rest = split(mm_split(split(basis * 0.25), inverse, ((1,), (0,))))
        back_ref[0] = head
        back_ref[1] = rest
        fill(own_ref[...])

    pl.when(pl.program_id(0) == 1)(lambda: fill(other_ref[...]))


def last_part(core, merged, own, other, right, inverse):
    width, cols = merged.shape
    half, rank = own.shape
    whole = lambda h, core: (0, 0)
    row = pl.BlockSpec((half, cols), lambda h, core: ((core[0] + h) % 2, 0))
    return pl.pallas_call(
        last_kernel,
        out_shape=(
            jax.ShapeDtypeStruct((width, cols), BF16),
            jax.ShapeDtypeStruct((cols, rank), F32),
        ),
        grid_spec=pltpu.PrefetchScalarGridSpec(
            num_scalar_prefetch=1,
            grid=(2,),
            in_specs=[
                row,
                pl.BlockSpec((half, rank), whole),
                pl.BlockSpec((half, rank), whole),
                pl.BlockSpec((cols, rank), whole),
                pl.BlockSpec((rank, rank), whole),
            ],
            out_specs=(row, pl.BlockSpec((cols, rank), whole)),
            scratch_shapes=[pltpu.VMEM((2, cols, rank), BF16)],
        ),
        compiler_params=params(),
        cost_estimate=pl.CostEstimate(flops=10**9, bytes_accessed=8 * 10**6, transcendentals=0),
    )(core, merged, own, other, right, inverse)


PLANE = ("z", "y", "c")
ALL = ("x", "z", "y", "c")


def swap(value, axis, bit):
    n = lax.axis_size(axis)
    return lax.ppermute(value, axis, [(i, i ^ bit) for i in range(n)])


def shift(value, axis, by):
    n = lax.axis_size(axis)
    return lax.ppermute(value, axis, [(i, (i + by) % n) for i in range(n)])


def pick(value, index):
    return lax.dynamic_index_in_dim(value, index, 0, keepdims=False)


def per_device(features, preact, upstream, weight, pairs, station_weight, counts, error, basis):
    tie = lax.optimization_barrier
    n_inter, n_z, n_y = lax.axis_size("x"), lax.axis_size("z"), lax.axis_size("y")
    group_rows, width = preact.shape[0], features.shape[1]
    rank, half = basis.shape[1], width // 2
    cols = preact.shape[1]
    c, y = lax.axis_index("c"), lax.axis_index("y")
    core = c.astype(jnp.int32)[None]

    all_features = lax.all_gather(features, PLANE, axis=0, tiled=True)
    give = lax.dynamic_slice_in_dim(features, (1 - c) * half, half, 1)
    keep = lax.dynamic_slice_in_dim(features, c * half, half, 1)
    got = swap(give, "c", 1)
    pair = jnp.where(c == 0, jnp.concatenate([keep, got]), jnp.concatenate([got, keep]))
    count = counts.astype(F32)
    count = count + swap(count, "x", 1)

    dpre, share = token_part(counts, pairs, station_weight, upstream, preact, basis)
    share = share + swap(share, "c", 1)
    count, share, error_late, late = tie((count, share, error, dpre))
    inv_mean = n_inter / (count + swap(count, "x", 2))
    err_give, err_keep = error_part(core, error_late, basis)
    err_got = swap(err_give, "c", 1)

    rows = late.reshape(n_z, n_y, 2, 8, cols).transpose(2, 1, 0, 3, 4).reshape(2, -1, cols)
    got = swap(mm(pick(rows, 1 - c), weight, ((1,), (1,))).astype(BF16), "c", 1)
    share = lax.all_to_all(share, ("z", "y"), 0, 0, tiled=True).reshape(n_z * n_y, -1, rank)
    grad = (mm(pick(rows, c), weight, ((1,), (1,))) + got.astype(F32)).astype(BF16)
    grad = grad.reshape(n_y, -1, width)
    piece = grad.shape[1] // 2
    far = pick(grad, (y + 2) % n_y)
    far_up, far_down = far[:piece], far[piece:]
    inv_mean, share, err_got, pair, grad, far_up, far_down = tie(
        (inv_mean, share, err_got, pair, grad, far_up, far_down)
    )
    part = left_part(inv_mean, share, pair, err_keep, err_got)

    up, down = shift(far_up, "y", 1), shift(far_down, "y", -1)
    after, before = pick(grad, (y + 1) % n_y), pick(grad, (y + 3) % n_y)
    after = jnp.concatenate([after[:piece] + up, after[piece:]])
    before = jnp.concatenate([before[:piece], before[piece:] + down])
    part = lax.all_to_all(part, ("x", "y"), 0, 0, tiled=True)
    after, before, part = tie((after, before, part))

    up, down = shift(after, "y", 1), shift(before, "y", -1)
    part = part.reshape(n_inter * n_y, -1, rank).sum(0)
    for bit in (1, 2, 4):
        part = part + swap(part, "z", bit)
    up, down, part = tie((up, down, part))

    mine = lax.all_to_all(
        jnp.broadcast_to(part[None], (n_inter * n_y,) + part.shape), ("x", "y"), 0, 0, tiled=True
    ).reshape(half, rank)
    merged, head, rest = merge_part(inv_mean, all_features, dpre, error)
    grad = pick(grad, y).astype(F32) + up.astype(F32) + down.astype(F32)
    grad = grad.astype(BF16)
    grad, merged, mine = tie((grad, merged, mine))

    other = swap(mine, "c", 1)
    gram = jnp.dot(mine.T, mine, precision=HIGHEST)
    gram, other = tie((gram, other))
    gram = gram + swap(gram, "c", 1)
    right = right_part(core, head, rest, mine, other)
    gram, grad, right = tie((gram, grad, right))
    right = right + swap(right, "x", 1)
    grad = lax.all_to_all(grad, "z", 0, 0, tiled=True)
    gram, right = tie((gram, right))
    inverse = inverse_part(gram)
    right = right + swap(right, "x", 2)
    new_error, new_basis = last_part(core, merged, mine, other, right, inverse)
    grad, new_basis = tie((grad, new_basis))
    grad = grad.reshape(n_z, -1, width).astype(F32).sum(0).astype(BF16)
    return grad, new_error, new_basis


def solution(mesh):
    mesh = Mesh(mesh.devices.reshape(4, 8, 4, 2), ALL)
    in_specs = (
        P(ALL, None),
        P("x", PLANE),
        P("x", PLANE),
        P(None, PLANE),
        P("x", None),
        P(),
        P("x"),
        P("x", PLANE),
        P(PLANE, None),
    )
    out_specs = (P(ALL, None), P("x", PLANE), P(PLANE, None))
    return jax.shard_map(
        per_device, mesh=mesh, in_specs=in_specs, out_specs=out_specs, check_vma=False
    )
```

```python
import functools, math
import jax
import jax.numpy as jnp
from jax import lax
from jax.experimental import pallas as pl
from jax.experimental.pallas import tpu as pltpu
from jax.sharding import Mesh, PartitionSpec as P

F32 = jnp.float32
BF16 = jnp.bfloat16
HIGHEST = lax.Precision.HIGHEST
VMEM = 56 * 1024 * 1024


def gelu_slope(value):
    cdf = 0.5 * (1.0 + lax.erf(value / math.sqrt(2.0)))
    return cdf + value * jnp.exp(-0.5 * value * value) / math.sqrt(2.0 * math.pi)


def split(value):
    head = value.astype(BF16)
    return head, (value - head.astype(F32)).astype(BF16)


def mm(a, b, contract):
    return lax.dot_general(a, b, (contract, ((), ())), preferred_element_type=F32)


def mm_wide(a, wide, contract):
    head, rest = split(wide)
    out = mm(a, jnp.concatenate([head, rest], axis=1), contract)
    n = wide.shape[1]
    return out[:, :n] + out[:, n:]


def mm_split(a, b, contract):
    return mm(a[0], b[0], contract) + (mm(a[0], b[1], contract) + mm(a[1], b[0], contract))


def params(limit=VMEM):
    return pltpu.CompilerParams(vmem_limit_bytes=limit)


def token_kernel(count_ref, pairs_ref, table_ref, up_ref, pre_ref, basis_ref, dpre_ref, rows_ref, share_ref):
    rows = up_ref.shape[0]
    stations = table_ref.shape[1]
    table = table_ref[...]
    head = table.astype(BF16)
    middle = (table - head.astype(F32)).astype(BF16)
    last = (table - head.astype(F32) - middle.astype(F32)).astype(BF16)
    which = lax.broadcasted_iota(jnp.int32, (stations, rows), 0)
    weight = None
    for end in range(2):
        onehot = (which == pairs_ref[end : end + 1, :]).astype(F32).astype(BF16)
        found = None
        for piece in (last, middle, head):
            term = mm(jnp.broadcast_to(piece, (16, stations)), onehot, ((1,), (0,)))[:1]
            found = term if found is None else found + term
        weight = found if weight is None else weight * found
    live = lax.broadcasted_iota(jnp.int32, (1, rows), 1) < count_ref[0]
    weight = jnp.where(live, weight, 0.0)
    column = jnp.transpose(jnp.broadcast_to(weight, (128, rows)))
    column = jnp.concatenate([column] * (up_ref.shape[1] // 128), axis=1)
    wide = up_ref[...].astype(F32) * gelu_slope(pre_ref[...].astype(F32)) * column
    dpre = wide.astype(BF16)
    dpre_ref[...] = dpre
    starts = [
        ((z * 4 + y) * 2 + core) * 8 for core in range(2) for y in range(4) for z in range(rows // 64)
    ]
    rows_ref[...] = jnp.concatenate([wide[s : s + 8] for s in starts], axis=0).astype(BF16)
    share_ref[...] = mm_wide(dpre, basis_ref[...], ((1,), (0,)))


def token_part(counts, pairs, table, upstream, preact, basis):
    vm = pl.BlockSpec(memory_space=pltpu.VMEM)
    return pl.pallas_call(
        token_kernel,
        out_shape=(
            jax.ShapeDtypeStruct(upstream.shape, BF16),
            jax.ShapeDtypeStruct(upstream.shape, BF16),
            jax.ShapeDtypeStruct((upstream.shape[0], basis.shape[1]), F32),
        ),
        in_specs=[pl.BlockSpec(memory_space=pltpu.SMEM)] + [vm] * 5,
        out_specs=(vm, vm, vm),
        compiler_params=params(),
        cost_estimate=pl.CostEstimate(flops=10**5, bytes_accessed=10**4, transcendentals=0),
    )(counts, pairs.T, table[None], upstream, preact, basis)


def err_kernel(core_ref, error_ref, basis_ref, give_ref, keep_ref):
    product = mm_wide(error_ref[...], basis_ref[...], ((1,), (0,)))

    @pl.when(pl.program_id(0) == 0)
    def _():
        give_ref[...] = product

    @pl.when(pl.program_id(0) == 1)
    def _():
        keep_ref[...] = product


def error_part(core, error, basis):
    rows, cols = error.shape
    rank, half = basis.shape[1], rows // 2
    whole = lambda h, core: (0, 0)
    return pl.pallas_call(
        err_kernel,
        out_shape=(jax.ShapeDtypeStruct((half, rank), F32),) * 2,
        grid_spec=pltpu.PrefetchScalarGridSpec(
            num_scalar_prefetch=1,
            grid=(2,),
            in_specs=[
                pl.BlockSpec((half, cols), lambda h, core: ((core[0] + 1 + h) % 2, 0)),
                pl.BlockSpec((cols, rank), whole),
            ],
            out_specs=(pl.BlockSpec((half, rank), whole),) * 2,
        ),
        compiler_params=params(),
        cost_estimate=pl.CostEstimate(flops=10**5, bytes_accessed=10**4, transcendentals=0),
    )(core, error, basis)


def left_kernel(inv_ref, share_ref, other_ref, feat_ref, keep_ref, got_ref, out_ref):
    share = share_ref[...] + other_ref[...]
    out_ref[...] = (
        keep_ref[...]
        + got_ref[...]
        + mm_wide(feat_ref[...], share * inv_ref[0], ((0,), (0,)))
    )


def left_part(inv_mean, share, share_got, feats, keep, got):
    tokens, rank = share.shape
    half = got.shape[0]
    step = half // 2
    rows = pl.BlockSpec((step, rank), lambda i: (i, 0))
    return pl.pallas_call(
        left_kernel,
        out_shape=jax.ShapeDtypeStruct((half, rank), F32),
        grid=(half // step,),
        in_specs=[
            pl.BlockSpec(memory_space=pltpu.SMEM),
            pl.BlockSpec((tokens, rank), lambda i: (0, 0)),
            pl.BlockSpec((tokens, rank), lambda i: (0, 0)),
            pl.BlockSpec((tokens, step), lambda i: (0, i)),
            rows,
            rows,
        ],
        out_specs=rows,
        compiler_params=params(),
        cost_estimate=pl.CostEstimate(flops=10**8, bytes_accessed=4 * 10**6, transcendentals=0),
    )(inv_mean, share, share_got, feats, keep, got)


def merge_kernel(inv_ref, feat_ref, dpre_ref, error_ref, merged_ref, head_ref, rest_ref):
    raw = mm(feat_ref[...], dpre_ref[...], ((0,), (0,)))
    merged = raw * inv_ref[0] + error_ref[...].astype(F32)
    merged_ref[...] = merged
    head, rest = split(jnp.transpose(merged))
    head_ref[...] = head
    rest_ref[...] = rest


def merge_part(inv_mean, features, dpre, error):
    tokens, width = features.shape
    cols = dpre.shape[1]
    step = 512
    return pl.pallas_call(
        merge_kernel,
        out_shape=(
            jax.ShapeDtypeStruct((width, cols), F32),
            jax.ShapeDtypeStruct((cols, width), BF16),
            jax.ShapeDtypeStruct((cols, width), BF16),
        ),
        grid=(width // step,),
        in_specs=[
            pl.BlockSpec(memory_space=pltpu.SMEM),
            pl.BlockSpec((tokens, step), lambda i: (0, i)),
            pl.BlockSpec((tokens, cols), lambda i: (0, 0)),
            pl.BlockSpec((step, cols), lambda i: (i, 0)),
        ],
        out_specs=(
            pl.BlockSpec((step, cols), lambda i: (i, 0)),
            pl.BlockSpec((cols, step), lambda i: (0, i)),
            pl.BlockSpec((cols, step), lambda i: (0, i)),
        ),
        compiler_params=params(),
        cost_estimate=pl.CostEstimate(flops=2 * 10**9, bytes_accessed=16 * 10**6, transcendentals=0),
    )(inv_mean, features, dpre, error)


def right_kernel(core_ref, head_ref, rest_ref, own_ref, other_ref, right_ref):
    def term(left):
        lh, ll = split(left)
        rank = lh.shape[1]
        both = mm(head_ref[...], jnp.concatenate([lh, ll], axis=1), ((1,), (0,)))
        return both[:, :rank] + both[:, rank:] + mm(rest_ref[...], lh, ((1,), (0,)))

    @pl.when(pl.program_id(0) == 0)
    def _():
        right_ref[...] = term(own_ref[...])

    @pl.when(pl.program_id(0) == 1)
    def _():
        right_ref[...] += term(other_ref[...])


def right_part(core, head, rest, own, other):
    cols, width = head.shape
    half, rank = own.shape
    whole = lambda h, core: (0, 0)
    column = pl.BlockSpec((cols, half), lambda h, core: (0, (core[0] + h) % 2))
    return pl.pallas_call(
        right_kernel,
        out_shape=jax.ShapeDtypeStruct((cols, rank), F32),
        grid_spec=pltpu.PrefetchScalarGridSpec(
            num_scalar_prefetch=1,
            grid=(2,),
            in_specs=[column, column] + [pl.BlockSpec((half, rank), whole)] * 2,
            out_specs=pl.BlockSpec((cols, rank), whole),
        ),
        compiler_params=params(),
        cost_estimate=pl.CostEstimate(flops=10**9, bytes_accessed=6 * 10**6, transcendentals=0),
    )(core, head, rest, own, other)


def inverse_kernel(gram_ref, out_ref):
    n = gram_ref.shape[0]
    a = gram_ref[...]
    b = (
        lax.broadcasted_iota(jnp.int32, (n, n), 0) == lax.broadcasted_iota(jnp.int32, (n, n), 1)
    ).astype(F32)
    for low in range(0, n, 8):
        left = n - low
        row_index = lax.broadcasted_iota(jnp.int32, (left, n), 0)
        columns = [
            jnp.broadcast_to(a[:, low + j : low + j + 1], (left, n)) for j in range(8)
        ]
        for j in range(8):
            column = columns[j]
            pivot = column[j : j + 1, :]
            scale = lax.rsqrt(pivot)
            scale = scale * (1.5 - 0.5 * pivot * scale * scale)
            row_a, row_b = a[j : j + 1, :], b[j : j + 1, :]
            out_ref[low + j : low + j + 1, :] = row_b * scale
            factor = jnp.where(row_index > j, column * (scale * scale), 0.0)
            for i in range(j + 1, 8):
                columns[i] = columns[i] - factor * column[i : i + 1, :]
            a = a - factor * row_a
            b = b - factor * row_b
        a, b = a[8:], b[8:]


def inverse_part(gram):
    vm = pl.BlockSpec(memory_space=pltpu.VMEM)
    return pl.pallas_call(
        inverse_kernel,
        out_shape=jax.ShapeDtypeStruct(gram.shape, F32),
        in_specs=[vm],
        out_specs=vm,
        compiler_params=params(VMEM // 8),
        cost_estimate=pl.CostEstimate(flops=10**7, bytes_accessed=10**5, transcendentals=128),
    )(gram)


def last_kernel(core_ref, merged_ref, own_ref, other_ref, right_ref, got_ref, inverse_ref, error_ref, basis_ref, back_ref):
    def fill(left):
        out = mm_split(split(left), (back_ref[0], back_ref[1]), ((1,), (1,)))
        error_ref[...] = (merged_ref[...] - out).astype(BF16)

    @pl.when(pl.program_id(0) == 0)
    def _():
        inverse = split(inverse_ref[...])
        basis = mm_split(split(right_ref[...] + got_ref[...]), inverse, ((1,), (1,)))
        basis_ref[...] = basis
        head, rest = split(mm_split(split(basis * 0.25), inverse, ((1,), (0,))))
        back_ref[0] = head
        back_ref[1] = rest
        fill(own_ref[...])

    pl.when(pl.program_id(0) == 1)(lambda: fill(other_ref[...]))


def last_part(core, merged, own, other, right, got, inverse):
    width, cols = merged.shape
    half, rank = own.shape
    whole = lambda h, core: (0, 0)
    row = pl.BlockSpec((half, cols), lambda h, core: ((core[0] + h) % 2, 0))
    return pl.pallas_call(
        last_kernel,
        out_shape=(
            jax.ShapeDtypeStruct((width, cols), BF16),
            jax.ShapeDtypeStruct((cols, rank), F32),
        ),
        grid_spec=pltpu.PrefetchScalarGridSpec(
            num_scalar_prefetch=1,
            grid=(2,),
            in_specs=[
                row,
                pl.BlockSpec((half, rank), whole),
                pl.BlockSpec((half, rank), whole),
                pl.BlockSpec((cols, rank), whole),
                pl.BlockSpec((cols, rank), whole),
                pl.BlockSpec((rank, rank), whole),
            ],
            out_specs=(row, pl.BlockSpec((cols, rank), whole)),
            scratch_shapes=[pltpu.VMEM((2, cols, rank), BF16)],
        ),
        compiler_params=params(),
        cost_estimate=pl.CostEstimate(flops=10**9, bytes_accessed=8 * 10**6, transcendentals=0),
    )(core, merged, own, other, right, got, inverse)


PLANE = ("z", "y", "c")
ALL = ("x", "z", "y", "c")


def swap(value, axis, bit):
    n = lax.axis_size(axis)
    return lax.ppermute(value, axis, [(i, i ^ bit) for i in range(n)])


def shift(value, axis, by):
    n = lax.axis_size(axis)
    return lax.ppermute(value, axis, [(i, (i + by) % n) for i in range(n)])


def pick(value, index):
    return lax.dynamic_index_in_dim(value, index, 0, keepdims=False)


def per_device(features, preact, upstream, weight, pairs, station_weight, counts, error, basis):
    tie = lax.optimization_barrier
    n_inter, n_z, n_y = lax.axis_size("x"), lax.axis_size("z"), lax.axis_size("y")
    group_rows, width = preact.shape[0], features.shape[1]
    rank, half = basis.shape[1], width // 2
    cols = preact.shape[1]
    c, y = lax.axis_index("c"), lax.axis_index("y")
    core = c.astype(jnp.int32)[None]

    all_features = lax.all_gather(features, PLANE, axis=0, tiled=True)
    give = lax.dynamic_slice_in_dim(features, (1 - c) * half, half, 1)
    keep = lax.dynamic_slice_in_dim(features, c * half, half, 1)
    got = swap(give, "c", 1)
    pair = jnp.where(c == 0, jnp.concatenate([keep, got]), jnp.concatenate([got, keep]))
    count = counts.astype(F32)
    count = count + swap(count, "x", 1)

    dpre, rows, share = token_part(counts, pairs, station_weight, upstream, preact, basis)
    count, share, error_late, rows = tie((count, share, error, rows))
    err_give, err_keep = error_part(core, error_late, basis)
    err_got = swap(err_give, "c", 1)
    inv_mean = n_inter / (count + swap(count, "x", 2))

    rows = rows.reshape(2, -1, cols)
    got = swap(mm(pick(rows, 1 - c), weight, ((1,), (1,))).astype(BF16), "c", 1)
    share = lax.all_to_all(share, ("z", "y"), 0, 0, tiled=True).reshape(n_z * n_y, -1, rank)
    grad = (mm(pick(rows, c), weight, ((1,), (1,))) + got.astype(F32)).astype(BF16)
    grad = grad.reshape(n_y, -1, width)
    piece = grad.shape[1] // 2
    far = pick(grad, (y + 2) % n_y)
    far_up, far_down = far[:piece], far[piece:]
    inv_mean, share, err_got, pair, grad, far_up, far_down = tie(
        (inv_mean, share, err_got, pair, grad, far_up, far_down)
    )
    share = share.sum(0)
    part = left_part(inv_mean, share, swap(share, "c", 1), pair, err_keep, err_got)

    up, down = shift(far_up, "y", 1), shift(far_down, "y", -1)
    grad, part = tie((grad, part))
    after, before = pick(grad, (y + 1) % n_y), pick(grad, (y + 3) % n_y)
    after = jnp.concatenate([after[:piece] + up, after[piece:]])
    before = jnp.concatenate([before[:piece], before[piece:] + down])
    part = lax.all_to_all(part, ("x", "y"), 0, 0, tiled=True)
    after, before, part = tie((after, before, part))

    up, down = shift(after, "y", 1), shift(before, "y", -1)
    part = part.reshape(n_inter * n_y, -1, rank).sum(0)
    for bit in (1, 2, 4):
        part = part + swap(part, "z", bit)
    up, down, part = tie((up, down, part))

    mine = lax.all_to_all(
        jnp.broadcast_to(part[None], (n_inter * n_y,) + part.shape), ("x", "y"), 0, 0, tiled=True
    ).reshape(half, rank)
    merged, head, rest = merge_part(inv_mean, all_features, dpre, error)
    grad = pick(grad, y).astype(F32) + up.astype(F32) + down.astype(F32)
    grad = grad.astype(BF16)
    grad, merged, mine = tie((grad, merged, mine))

    other = swap(mine, "c", 1)
    grad = lax.all_to_all(grad, "z", 0, 0, tiled=True)
    gram = jnp.dot(mine.T, mine, precision=HIGHEST)
    gram = gram + swap(gram, "c", 1)
    gram, other = tie((gram, other))
    right = right_part(core, head, rest, mine, other)
    inverse = inverse_part(gram)
    right = right + swap(right, "x", 1)
    inverse, right = tie((inverse, right))
    right_got = swap(right, "x", 2)
    grad = grad.reshape(n_z, -1, width).astype(F32).sum(0).astype(BF16)
    grad, right_got = tie((grad, right_got))
    new_error, new_basis = last_part(core, merged, mine, other, right, right_got, inverse)
    return grad, new_error, new_basis


def solution(mesh):
    mesh = Mesh(mesh.devices.reshape(4, 8, 4, 2), ALL)
    in_specs = (
        P(ALL, None),
        P("x", PLANE),
        P("x", PLANE),
        P(None, PLANE),
        P("x", None),
        P(),
        P("x"),
        P("x", PLANE),
        P(PLANE, None),
    )
    out_specs = (P(ALL, None), P("x", PLANE), P(PLANE, None))
    return jax.shard_map(
        per_device, mesh=mesh, in_specs=in_specs, out_specs=out_specs, check_vma=False
    )
```

```python
import functools, math
import jax
import jax.numpy as jnp
from jax import lax
from jax.experimental import pallas as pl
from jax.experimental.pallas import tpu as pltpu
from jax.sharding import Mesh, PartitionSpec as P

F32 = jnp.float32
BF16 = jnp.bfloat16
HIGHEST = lax.Precision.HIGHEST
VMEM = 56 * 1024 * 1024


def gelu_slope(value):
    cdf = 0.5 * (1.0 + lax.erf(value / math.sqrt(2.0)))
    return cdf + value * jnp.exp(-0.5 * value * value) / math.sqrt(2.0 * math.pi)


def split(value):
    head = value.astype(BF16)
    return head, (value - head.astype(F32)).astype(BF16)


def mm(a, b, contract):
    return lax.dot_general(a, b, (contract, ((), ())), preferred_element_type=F32)


def mm_wide(a, wide, contract):
    head, rest = split(wide)
    out = mm(a, jnp.concatenate([head, rest], axis=1), contract)
    n = wide.shape[1]
    return out[:, :n] + out[:, n:]


def mm_split(a, b, contract):
    return mm(a[0], b[0], contract) + (mm(a[0], b[1], contract) + mm(a[1], b[0], contract))


def params(limit=VMEM):
    return pltpu.CompilerParams(vmem_limit_bytes=limit)


def token_kernel(count_ref, pairs_ref, table_ref, up_ref, pre_ref, basis_ref, dpre_ref, rows_ref, share_ref):
    rows = up_ref.shape[0]
    stations = table_ref.shape[1]
    table = table_ref[...]
    head = table.astype(BF16)
    middle = (table - head.astype(F32)).astype(BF16)
    last = (table - head.astype(F32) - middle.astype(F32)).astype(BF16)
    which = lax.broadcasted_iota(jnp.int32, (stations, rows), 0)
    weight = None
    for end in range(2):
        onehot = (which == pairs_ref[end : end + 1, :]).astype(F32).astype(BF16)
        found = None
        for piece in (last, middle, head):
            term = mm(jnp.broadcast_to(piece, (16, stations)), onehot, ((1,), (0,)))[:1]
            found = term if found is None else found + term
        weight = found if weight is None else weight * found
    live = lax.broadcasted_iota(jnp.int32, (1, rows), 1) < count_ref[0]
    weight = jnp.where(live, weight, 0.0)
    column = jnp.transpose(jnp.broadcast_to(weight, (128, rows)))
    column = jnp.concatenate([column] * (up_ref.shape[1] // 128), axis=1)
    wide = up_ref[...].astype(F32) * gelu_slope(pre_ref[...].astype(F32)) * column
    dpre = wide.astype(BF16)
    dpre_ref[...] = dpre
    starts = [
        ((z * 4 + y) * 2 + core) * 8 for core in range(2) for y in range(4) for z in range(rows // 64)
    ]
    rows_ref[...] = jnp.concatenate([wide[s : s + 8] for s in starts], axis=0).astype(BF16)
    share_ref[...] = mm_wide(dpre, basis_ref[...], ((1,), (0,)))


def token_part(counts, pairs, table, upstream, preact, basis):
    vm = pl.BlockSpec(memory_space=pltpu.VMEM)
    return pl.pallas_call(
        token_kernel,
        out_shape=(
            jax.ShapeDtypeStruct(upstream.shape, BF16),
            jax.ShapeDtypeStruct(upstream.shape, BF16),
            jax.ShapeDtypeStruct((upstream.shape[0], basis.shape[1]), F32),
        ),
        in_specs=[pl.BlockSpec(memory_space=pltpu.SMEM)] + [vm] * 5,
        out_specs=(vm, vm, vm),
        compiler_params=params(),
        cost_estimate=pl.CostEstimate(flops=10**5, bytes_accessed=10**4, transcendentals=0),
    )(counts, pairs.T, table[None], upstream, preact, basis)


def err_kernel(core_ref, error_ref, basis_ref, give_ref, keep_ref):
    product = mm_wide(error_ref[...], basis_ref[...], ((1,), (0,)))

    @pl.when(pl.program_id(0) == 0)
    def _():
        give_ref[...] = product

    @pl.when(pl.program_id(0) == 1)
    def _():
        keep_ref[...] = product


def error_part(core, error, basis):
    rows, cols = error.shape
    rank, half = basis.shape[1], rows // 2
    whole = lambda h, core: (0, 0)
    return pl.pallas_call(
        err_kernel,
        out_shape=(jax.ShapeDtypeStruct((half, rank), F32),) * 2,
        grid_spec=pltpu.PrefetchScalarGridSpec(
            num_scalar_prefetch=1,
            grid=(2,),
            in_specs=[
                pl.BlockSpec((half, cols), lambda h, core: ((core[0] + 1 + h) % 2, 0)),
                pl.BlockSpec((cols, rank), whole),
            ],
            out_specs=(pl.BlockSpec((half, rank), whole),) * 2,
        ),
        compiler_params=params(),
        cost_estimate=pl.CostEstimate(flops=10**5, bytes_accessed=10**4, transcendentals=0),
    )(core, error, basis)


def left_kernel(inv_ref, share_ref, other_ref, feat_ref, keep_ref, got_ref, out_ref):
    share = share_ref[...] + other_ref[...]
    out_ref[...] = (
        keep_ref[...]
        + got_ref[...]
        + mm_wide(feat_ref[...], share * inv_ref[0], ((0,), (0,)))
    )


def left_part(inv_mean, share, share_got, feats, keep, got):
    tokens, rank = share.shape
    half = got.shape[0]
    step = half // 2
    rows = pl.BlockSpec((step, rank), lambda i: (i, 0))
    return pl.pallas_call(
        left_kernel,
        out_shape=jax.ShapeDtypeStruct((half, rank), F32),
        grid=(half // step,),
        in_specs=[
            pl.BlockSpec(memory_space=pltpu.SMEM),
            pl.BlockSpec((tokens, rank), lambda i: (0, 0)),
            pl.BlockSpec((tokens, rank), lambda i: (0, 0)),
            pl.BlockSpec((tokens, step), lambda i: (0, i)),
            rows,
            rows,
        ],
        out_specs=rows,
        compiler_params=params(),
        cost_estimate=pl.CostEstimate(flops=10**8, bytes_accessed=4 * 10**6, transcendentals=0),
    )(inv_mean, share, share_got, feats, keep, got)


def merge_kernel(inv_ref, feat_ref, dpre_ref, error_ref, merged_ref, head_ref, rest_ref):
    raw = mm(feat_ref[...], dpre_ref[...], ((0,), (0,)))
    merged = raw * inv_ref[0] + error_ref[...].astype(F32)
    merged_ref[...] = merged
    head, rest = split(jnp.transpose(merged))
    head_ref[...] = head
    rest_ref[...] = rest


def merge_part(inv_mean, features, dpre, error):
    tokens, width = features.shape
    cols = dpre.shape[1]
    step = 2048
    return pl.pallas_call(
        merge_kernel,
        out_shape=(
            jax.ShapeDtypeStruct((width, cols), F32),
            jax.ShapeDtypeStruct((cols, width), BF16),
            jax.ShapeDtypeStruct((cols, width), BF16),
        ),
        grid=(width // step,),
        in_specs=[
            pl.BlockSpec(memory_space=pltpu.SMEM),
            pl.BlockSpec((tokens, step), lambda i: (0, i)),
            pl.BlockSpec((tokens, cols), lambda i: (0, 0)),
            pl.BlockSpec((step, cols), lambda i: (i, 0)),
        ],
        out_specs=(
            pl.BlockSpec((step, cols), lambda i: (i, 0)),
            pl.BlockSpec((cols, step), lambda i: (0, i)),
            pl.BlockSpec((cols, step), lambda i: (0, i)),
        ),
        compiler_params=params(),
        cost_estimate=pl.CostEstimate(flops=2 * 10**9, bytes_accessed=16 * 10**6, transcendentals=0),
    )(inv_mean, features, dpre, error)


def right_kernel(core_ref, head_ref, rest_ref, own_ref, other_ref, right_ref):
    def term(left):
        lh, ll = split(left)
        rank = lh.shape[1]
        both = mm(head_ref[...], jnp.concatenate([lh, ll], axis=1), ((1,), (0,)))
        return both[:, :rank] + both[:, rank:] + mm(rest_ref[...], lh, ((1,), (0,)))

    @pl.when(pl.program_id(0) == 0)
    def _():
        right_ref[...] = term(own_ref[...])

    @pl.when(pl.program_id(0) == 1)
    def _():
        right_ref[...] += term(other_ref[...])


def right_part(core, head, rest, own, other):
    cols, width = head.shape
    half, rank = own.shape
    whole = lambda h, core: (0, 0)
    column = pl.BlockSpec((cols, half), lambda h, core: (0, (core[0] + h) % 2))
    return pl.pallas_call(
        right_kernel,
        out_shape=jax.ShapeDtypeStruct((cols, rank), F32),
        grid_spec=pltpu.PrefetchScalarGridSpec(
            num_scalar_prefetch=1,
            grid=(2,),
            in_specs=[column, column] + [pl.BlockSpec((half, rank), whole)] * 2,
            out_specs=pl.BlockSpec((cols, rank), whole),
        ),
        compiler_params=params(),
        cost_estimate=pl.CostEstimate(flops=10**9, bytes_accessed=6 * 10**6, transcendentals=0),
    )(core, head, rest, own, other)


def inverse_kernel(gram_ref, out_ref):
    n = gram_ref.shape[0]
    a = gram_ref[...]
    b = (
        lax.broadcasted_iota(jnp.int32, (n, n), 0) == lax.broadcasted_iota(jnp.int32, (n, n), 1)
    ).astype(F32)
    for low in range(0, n, 8):
        left = n - low
        row_index = lax.broadcasted_iota(jnp.int32, (left, n), 0)
        columns = [
            jnp.broadcast_to(a[:, low + j : low + j + 1], (left, n)) for j in range(8)
        ]
        for j in range(8):
            column = columns[j]
            pivot = column[j : j + 1, :]
            scale = lax.rsqrt(pivot)
            scale = scale * (1.5 - 0.5 * pivot * scale * scale)
            row_a, row_b = a[j : j + 1, :], b[j : j + 1, :]
            out_ref[low + j : low + j + 1, :] = row_b * scale
            factor = jnp.where(row_index > j, column * (scale * scale), 0.0)
            for i in range(j + 1, 8):
                columns[i] = columns[i] - factor * column[i : i + 1, :]
            a = a - factor * row_a
            b = b - factor * row_b
        a, b = a[8:], b[8:]


def inverse_part(gram):
    vm = pl.BlockSpec(memory_space=pltpu.VMEM)
    return pl.pallas_call(
        inverse_kernel,
        out_shape=jax.ShapeDtypeStruct(gram.shape, F32),
        in_specs=[vm],
        out_specs=vm,
        compiler_params=params(VMEM // 8),
        cost_estimate=pl.CostEstimate(flops=10**7, bytes_accessed=10**5, transcendentals=128),
    )(gram)


def last_kernel(core_ref, merged_ref, own_ref, other_ref, right_ref, got_ref, inverse_ref, error_ref, basis_ref, back_ref):
    def fill(left):
        out = mm_split(split(left), (back_ref[0], back_ref[1]), ((1,), (1,)))
        error_ref[...] = (merged_ref[...] - out).astype(BF16)

    @pl.when(pl.program_id(0) == 0)
    def _():
        inverse = split(inverse_ref[...])
        basis = mm_split(split(right_ref[...] + got_ref[...]), inverse, ((1,), (1,)))
        basis_ref[...] = basis
        head, rest = split(mm_split(split(basis * 0.25), inverse, ((1,), (0,))))
        back_ref[0] = head
        back_ref[1] = rest
        fill(own_ref[...])

    pl.when(pl.program_id(0) == 1)(lambda: fill(other_ref[...]))


def last_part(core, merged, own, other, right, got, inverse):
    width, cols = merged.shape
    half, rank = own.shape
    whole = lambda h, core: (0, 0)
    row = pl.BlockSpec((half, cols), lambda h, core: ((core[0] + h) % 2, 0))
    return pl.pallas_call(
        last_kernel,
        out_shape=(
            jax.ShapeDtypeStruct((width, cols), BF16),
            jax.ShapeDtypeStruct((cols, rank), F32),
        ),
        grid_spec=pltpu.PrefetchScalarGridSpec(
            num_scalar_prefetch=1,
            grid=(2,),
            in_specs=[
                row,
                pl.BlockSpec((half, rank), whole),
                pl.BlockSpec((half, rank), whole),
                pl.BlockSpec((cols, rank), whole),
                pl.BlockSpec((cols, rank), whole),
                pl.BlockSpec((rank, rank), whole),
            ],
            out_specs=(row, pl.BlockSpec((cols, rank), whole)),
            scratch_shapes=[pltpu.VMEM((2, cols, rank), BF16)],
        ),
        compiler_params=params(),
        cost_estimate=pl.CostEstimate(flops=10**9, bytes_accessed=8 * 10**6, transcendentals=0),
    )(core, merged, own, other, right, got, inverse)


PLANE = ("z", "y", "c")
ALL = ("x", "z", "y", "c")


def swap(value, axis, bit):
    n = lax.axis_size(axis)
    return lax.ppermute(value, axis, [(i, i ^ bit) for i in range(n)])


def shift(value, axis, by):
    n = lax.axis_size(axis)
    return lax.ppermute(value, axis, [(i, (i + by) % n) for i in range(n)])


def pick(value, index):
    return lax.dynamic_index_in_dim(value, index, 0, keepdims=False)


def per_device(features, preact, upstream, weight, pairs, station_weight, counts, error, basis):
    tie = lax.optimization_barrier
    n_inter, n_z, n_y = lax.axis_size("x"), lax.axis_size("z"), lax.axis_size("y")
    group_rows, width = preact.shape[0], features.shape[1]
    rank, half = basis.shape[1], width // 2
    cols = preact.shape[1]
    c, y = lax.axis_index("c"), lax.axis_index("y")
    core = c.astype(jnp.int32)[None]

    all_features = lax.all_gather(features, PLANE, axis=0, tiled=True)
    give = lax.dynamic_slice_in_dim(features, (1 - c) * half, half, 1)
    keep = lax.dynamic_slice_in_dim(features, c * half, half, 1)
    got = swap(give, "c", 1)
    pair = jnp.where(c == 0, jnp.concatenate([keep, got]), jnp.concatenate([got, keep]))
    count = counts.astype(F32)
    count = count + swap(count, "x", 1)

    dpre, rows, share = token_part(counts, pairs, station_weight, upstream, preact, basis)
    count, share, error_late, rows = tie((count, share, error, rows))
    err_give, err_keep = error_part(core, error_late, basis)
    err_got = swap(err_give, "c", 1)
    inv_mean = n_inter / (count + swap(count, "x", 3))

    rows = rows.reshape(2, -1, cols)
    got = swap(mm(pick(rows, 1 - c), weight, ((1,), (1,))).astype(BF16), "c", 1)
    share = lax.all_to_all(share, ("z", "y"), 0, 0, tiled=True).reshape(n_z * n_y, -1, rank)
    grad = (mm(pick(rows, c), weight, ((1,), (1,))) + got.astype(F32)).astype(BF16)
    grad = grad.reshape(n_y, -1, width)
    piece = grad.shape[1] // 2
    far = pick(grad, (y + 2) % n_y)
    far_up, far_down = far[:piece], far[piece:]
    inv_mean, share, err_got, pair, grad, far_up, far_down = tie(
        (inv_mean, share, err_got, pair, grad, far_up, far_down)
    )
    share = share.sum(0)
    part = left_part(inv_mean, share, swap(share, "c", 1), pair, err_keep, err_got)

    up, down = shift(far_up, "y", 1), shift(far_down, "y", -1)
    grad, part = tie((grad, part))
    after, before = pick(grad, (y + 1) % n_y), pick(grad, (y + 3) % n_y)
    after = jnp.concatenate([after[:piece] + up, after[piece:]])
    before = jnp.concatenate([before[:piece], before[piece:] + down])
    part = lax.all_to_all(part, ("x", "y"), 0, 0, tiled=True)
    after, before, part = tie((after, before, part))

    up, down = shift(after, "y", 1), shift(before, "y", -1)
    part = part.reshape(n_inter * n_y, -1, rank).sum(0)
    for bit in (1, 2, 7):
        part = part + swap(part, "z", bit)
    up, down, part = tie((up, down, part))

    mine = lax.all_to_all(
        jnp.broadcast_to(part[None], (n_inter * n_y,) + part.shape), ("x", "y"), 0, 0, tiled=True
    ).reshape(half, rank)
    merged, head, rest = merge_part(inv_mean, all_features, dpre, error)
    grad = pick(grad, y).astype(F32) + up.astype(F32) + down.astype(F32)
    grad = grad.astype(BF16)
    grad, merged, mine = tie((grad, merged, mine))

    other = swap(mine, "c", 1)
    grad = lax.all_to_all(grad, "z", 0, 0, tiled=True)
    right = right_part(core, head, rest, mine, other)
    right_got = swap(right, "x", 1)
    right, mine = tie((right, mine))
    gram = jnp.dot(mine.T, mine, precision=HIGHEST)
    gram = gram + swap(gram, "c", 1)
    gram, right = tie((gram, right + right_got))
    right_got = swap(right, "x", 3)
    inverse = inverse_part(gram)
    new_error, new_basis = last_part(core, merged, mine, other, right, right_got, inverse)
    grad, new_basis = tie((grad, new_basis))
    grad = grad.reshape(n_z, -1, width).astype(F32).sum(0).astype(BF16)
    return grad, new_error, new_basis


def solution(mesh):
    mesh = Mesh(mesh.devices.reshape(4, 8, 4, 2), ALL)
    in_specs = (
        P(ALL, None),
        P("x", PLANE),
        P("x", PLANE),
        P(None, PLANE),
        P("x", None),
        P(),
        P("x"),
        P("x", PLANE),
        P(PLANE, None),
    )
    out_specs = (P(ALL, None), P("x", PLANE), P(PLANE, None))
    return jax.shard_map(
        per_device, mesh=mesh, in_specs=in_specs, out_specs=out_specs, check_vma=False
    )
```

```python
import functools, math
import jax
import jax.numpy as jnp
from jax import lax
from jax.experimental import pallas as pl
from jax.experimental.pallas import tpu as pltpu
from jax.sharding import Mesh, PartitionSpec as P

F32 = jnp.float32
BF16 = jnp.bfloat16
HIGHEST = lax.Precision.HIGHEST
VMEM = 56 * 1024 * 1024


def gelu_slope(value):
    cdf = 0.5 * (1.0 + lax.erf(value / math.sqrt(2.0)))
    return cdf + value * jnp.exp(-0.5 * value * value) / math.sqrt(2.0 * math.pi)


def split(value):
    head = value.astype(BF16)
    return head, (value - head.astype(F32)).astype(BF16)


def mm(a, b, contract):
    return lax.dot_general(a, b, (contract, ((), ())), preferred_element_type=F32)


def mm_wide(a, wide, contract):
    head, rest = split(wide)
    out = mm(a, jnp.concatenate([head, rest], axis=1), contract)
    n = wide.shape[1]
    return out[:, :n] + out[:, n:]


def mm_split(a, b, contract):
    return mm(a[0], b[0], contract) + (mm(a[0], b[1], contract) + mm(a[1], b[0], contract))


def params(limit=VMEM):
    return pltpu.CompilerParams(vmem_limit_bytes=limit)


def token_kernel(count_ref, pairs_ref, table_ref, up_ref, pre_ref, basis_ref, dpre_ref, rows_ref, share_ref):
    rows = up_ref.shape[0]
    stations = table_ref.shape[1]
    table = table_ref[...]
    head = table.astype(BF16)
    middle = (table - head.astype(F32)).astype(BF16)
    last = (table - head.astype(F32) - middle.astype(F32)).astype(BF16)
    which = lax.broadcasted_iota(jnp.int32, (stations, rows), 0)
    weight = None
    for end in range(2):
        onehot = (which == pairs_ref[end : end + 1, :]).astype(F32).astype(BF16)
        found = None
        for piece in (last, middle, head):
            term = mm(jnp.broadcast_to(piece, (16, stations)), onehot, ((1,), (0,)))[:1]
            found = term if found is None else found + term
        weight = found if weight is None else weight * found
    live = lax.broadcasted_iota(jnp.int32, (1, rows), 1) < count_ref[0]
    weight = jnp.where(live, weight, 0.0)
    column = jnp.transpose(jnp.broadcast_to(weight, (128, rows)))
    column = jnp.concatenate([column] * (up_ref.shape[1] // 128), axis=1)
    wide = up_ref[...].astype(F32) * gelu_slope(pre_ref[...].astype(F32)) * column
    dpre = wide.astype(BF16)
    dpre_ref[...] = dpre
    starts = [
        ((z * 4 + y) * 2 + core) * 8 for core in range(2) for y in range(4) for z in range(rows // 64)
    ]
    rows_ref[...] = jnp.concatenate([wide[s : s + 8] for s in starts], axis=0).astype(BF16)
    share_ref[...] = mm_wide(dpre, basis_ref[...], ((1,), (0,)))


def token_part(counts, pairs, table, upstream, preact, basis):
    vm = pl.BlockSpec(memory_space=pltpu.VMEM)
    return pl.pallas_call(
        token_kernel,
        out_shape=(
            jax.ShapeDtypeStruct(upstream.shape, BF16),
            jax.ShapeDtypeStruct(upstream.shape, BF16),
            jax.ShapeDtypeStruct((upstream.shape[0], basis.shape[1]), F32),
        ),
        in_specs=[pl.BlockSpec(memory_space=pltpu.SMEM)] + [vm] * 5,
        out_specs=(vm, vm, vm),
        compiler_params=params(),
        cost_estimate=pl.CostEstimate(flops=10**5, bytes_accessed=10**4, transcendentals=0),
    )(counts, pairs.T, table[None], upstream, preact, basis)


def err_kernel(core_ref, error_ref, basis_ref, give_ref, keep_ref):
    product = mm_wide(error_ref[...], basis_ref[...], ((1,), (0,)))

    @pl.when(pl.program_id(0) == 0)
    def _():
        give_ref[...] = product

    @pl.when(pl.program_id(0) == 1)
    def _():
        keep_ref[...] = product


def error_part(core, error, basis):
    rows, cols = error.shape
    rank, half = basis.shape[1], rows // 2
    whole = lambda h, core: (0, 0)
    return pl.pallas_call(
        err_kernel,
        out_shape=(jax.ShapeDtypeStruct((half, rank), F32),) * 2,
        grid_spec=pltpu.PrefetchScalarGridSpec(
            num_scalar_prefetch=1,
            grid=(2,),
            in_specs=[
                pl.BlockSpec((half, cols), lambda h, core: ((core[0] + 1 + h) % 2, 0)),
                pl.BlockSpec((cols, rank), whole),
            ],
            out_specs=(pl.BlockSpec((half, rank), whole),) * 2,
        ),
        compiler_params=params(),
        cost_estimate=pl.CostEstimate(flops=10**5, bytes_accessed=10**4, transcendentals=0),
    )(core, error, basis)


def left_kernel(inv_ref, share_ref, other_ref, feat_ref, keep_ref, got_ref, out_ref):
    share = share_ref[...] + other_ref[...]
    out_ref[...] = (
        keep_ref[...]
        + got_ref[...]
        + mm_wide(feat_ref[...], share * inv_ref[0], ((0,), (0,)))
    )


def left_part(inv_mean, share, share_got, feats, keep, got):
    tokens, rank = share.shape
    half = got.shape[0]
    step = half
    rows = pl.BlockSpec((step, rank), lambda i: (i, 0))
    return pl.pallas_call(
        left_kernel,
        out_shape=jax.ShapeDtypeStruct((half, rank), F32),
        grid=(half // step,),
        in_specs=[
            pl.BlockSpec(memory_space=pltpu.SMEM),
            pl.BlockSpec((tokens, rank), lambda i: (0, 0)),
            pl.BlockSpec((tokens, rank), lambda i: (0, 0)),
            pl.BlockSpec((tokens, step), lambda i: (0, i)),
            rows,
            rows,
        ],
        out_specs=rows,
        compiler_params=params(VMEM // 4),
        cost_estimate=pl.CostEstimate(flops=10**8, bytes_accessed=4 * 10**6, transcendentals=0),
    )(inv_mean, share, share_got, feats, keep, got)


def merge_kernel(inv_ref, feat_ref, dpre_ref, error_ref, merged_ref, head_ref, rest_ref):
    raw = mm(feat_ref[...], dpre_ref[...], ((0,), (0,)))
    merged = raw * inv_ref[0] + error_ref[...].astype(F32)
    merged_ref[...] = merged
    head, rest = split(jnp.transpose(merged))
    head_ref[...] = head
    rest_ref[...] = rest


def merge_part(inv_mean, features, dpre, error):
    tokens, width = features.shape
    cols = dpre.shape[1]
    step = 2048
    return pl.pallas_call(
        merge_kernel,
        out_shape=(
            jax.ShapeDtypeStruct((width, cols), F32),
            jax.ShapeDtypeStruct((cols, width), BF16),
            jax.ShapeDtypeStruct((cols, width), BF16),
        ),
        grid=(width // step,),
        in_specs=[
            pl.BlockSpec(memory_space=pltpu.SMEM),
            pl.BlockSpec((tokens, step), lambda i: (0, i)),
            pl.BlockSpec((tokens, cols), lambda i: (0, 0)),
            pl.BlockSpec((step, cols), lambda i: (i, 0)),
        ],
        out_specs=(
            pl.BlockSpec((step, cols), lambda i: (i, 0)),
            pl.BlockSpec((cols, step), lambda i: (0, i)),
            pl.BlockSpec((cols, step), lambda i: (0, i)),
        ),
        compiler_params=params(),
        cost_estimate=pl.CostEstimate(flops=2 * 10**9, bytes_accessed=16 * 10**6, transcendentals=0),
    )(inv_mean, features, dpre, error)


def right_kernel(core_ref, head_ref, rest_ref, own_ref, other_ref, right_ref):
    def term(left):
        lh, ll = split(left)
        rank = lh.shape[1]
        both = mm(head_ref[...], jnp.concatenate([lh, ll], axis=1), ((1,), (0,)))
        return both[:, :rank] + both[:, rank:] + mm(rest_ref[...], lh, ((1,), (0,)))

    @pl.when(pl.program_id(0) == 0)
    def _():
        right_ref[...] = term(own_ref[...])

    @pl.when(pl.program_id(0) == 1)
    def _():
        right_ref[...] += term(other_ref[...])


def right_part(core, head, rest, own, other):
    cols, width = head.shape
    half, rank = own.shape
    whole = lambda h, core: (0, 0)
    column = pl.BlockSpec((cols, half), lambda h, core: (0, (core[0] + h) % 2))
    return pl.pallas_call(
        right_kernel,
        out_shape=jax.ShapeDtypeStruct((cols, rank), F32),
        grid_spec=pltpu.PrefetchScalarGridSpec(
            num_scalar_prefetch=1,
            grid=(2,),
            in_specs=[column, column] + [pl.BlockSpec((half, rank), whole)] * 2,
            out_specs=pl.BlockSpec((cols, rank), whole),
        ),
        compiler_params=params(),
        cost_estimate=pl.CostEstimate(flops=10**9, bytes_accessed=6 * 10**6, transcendentals=0),
    )(core, head, rest, own, other)


def inverse_kernel(gram_ref, out_ref):
    n = gram_ref.shape[0]
    a = gram_ref[...]
    b = (
        lax.broadcasted_iota(jnp.int32, (n, n), 0) == lax.broadcasted_iota(jnp.int32, (n, n), 1)
    ).astype(F32)
    for low in range(0, n, 8):
        left = n - low
        row_index = lax.broadcasted_iota(jnp.int32, (left, n), 0)
        columns = [
            jnp.broadcast_to(a[:, low + j : low + j + 1], (left, n)) for j in range(8)
        ]
        for j in range(8):
            column = columns[j]
            pivot = column[j : j + 1, :]
            scale = lax.rsqrt(pivot)
            scale = scale * (1.5 - 0.5 * pivot * scale * scale)
            row_a, row_b = a[j : j + 1, :], b[j : j + 1, :]
            out_ref[low + j : low + j + 1, :] = row_b * scale
            factor = jnp.where(row_index > j, column * (scale * scale), 0.0)
            for i in range(j + 1, 8):
                columns[i] = columns[i] - factor * column[i : i + 1, :]
            a = a - factor * row_a
            b = b - factor * row_b
        a, b = a[8:], b[8:]


def inverse_part(gram):
    vm = pl.BlockSpec(memory_space=pltpu.VMEM)
    return pl.pallas_call(
        inverse_kernel,
        out_shape=jax.ShapeDtypeStruct(gram.shape, F32),
        in_specs=[vm],
        out_specs=vm,
        compiler_params=params(VMEM // 8),
        cost_estimate=pl.CostEstimate(flops=10**7, bytes_accessed=10**5, transcendentals=128),
    )(gram)


def last_kernel(core_ref, merged_ref, own_ref, other_ref, right_ref, got_ref, inverse_ref, grad_ref, error_ref, basis_ref, sum_ref, back_ref):
    def fill(left):
        out = mm_split(split(left), (back_ref[0], back_ref[1]), ((1,), (1,)))
        error_ref[...] = (merged_ref[...] - out).astype(BF16)

    @pl.when(pl.program_id(0) == 0)
    def _():
        inverse = split(inverse_ref[...])
        basis = mm_split(split(right_ref[...] + got_ref[...]), inverse, ((1,), (1,)))
        basis_ref[...] = basis
        head, rest = split(mm_split(split(basis * 0.25), inverse, ((1,), (0,))))
        back_ref[0] = head
        back_ref[1] = rest
        fill(own_ref[...])
        rows, step = sum_ref.shape[0], 512
        for start in range(0, sum_ref.shape[1], step):
            blocks = grad_ref[:, start : start + step].astype(F32)
            total = blocks[:rows]
            for first in range(rows, blocks.shape[0], rows):
                total = total + blocks[first : first + rows]
            sum_ref[:, start : start + step] = total.astype(BF16)

    pl.when(pl.program_id(0) == 1)(lambda: fill(other_ref[...]))


def last_part(core, merged, own, other, right, got, inverse, grad):
    width, cols = merged.shape
    half, rank = own.shape
    whole = lambda h, core: (0, 0)
    row = pl.BlockSpec((half, cols), lambda h, core: ((core[0] + h) % 2, 0))
    return pl.pallas_call(
        last_kernel,
        out_shape=(
            jax.ShapeDtypeStruct((width, cols), BF16),
            jax.ShapeDtypeStruct((cols, rank), F32),
            jax.ShapeDtypeStruct((8, grad.shape[1]), BF16),
        ),
        grid_spec=pltpu.PrefetchScalarGridSpec(
            num_scalar_prefetch=1,
            grid=(2,),
            in_specs=[
                row,
                pl.BlockSpec((half, rank), whole),
                pl.BlockSpec((half, rank), whole),
                pl.BlockSpec((cols, rank), whole),
                pl.BlockSpec((cols, rank), whole),
                pl.BlockSpec((rank, rank), whole),
                pl.BlockSpec(grad.shape, whole),
            ],
            out_specs=(
                row,
                pl.BlockSpec((cols, rank), whole),
                pl.BlockSpec((8, grad.shape[1]), whole),
            ),
            scratch_shapes=[pltpu.VMEM((2, cols, rank), BF16)],
        ),
        compiler_params=params(),
        cost_estimate=pl.CostEstimate(flops=10**9, bytes_accessed=8 * 10**6, transcendentals=0),
    )(core, merged, own, other, right, got, inverse, grad)


PLANE = ("z", "y", "c")
ALL = ("x", "z", "y", "c")


def swap(value, axis, bit):
    n = lax.axis_size(axis)
    return lax.ppermute(value, axis, [(i, i ^ bit) for i in range(n)])


def shift(value, axis, by):
    n = lax.axis_size(axis)
    return lax.ppermute(value, axis, [(i, (i + by) % n) for i in range(n)])


def pick(value, index):
    return lax.dynamic_index_in_dim(value, index, 0, keepdims=False)


def per_device(features, preact, upstream, weight, pairs, station_weight, counts, error, basis):
    tie = lax.optimization_barrier
    n_inter, n_z, n_y = lax.axis_size("x"), lax.axis_size("z"), lax.axis_size("y")
    group_rows, width = preact.shape[0], features.shape[1]
    rank, half = basis.shape[1], width // 2
    cols = preact.shape[1]
    c, y = lax.axis_index("c"), lax.axis_index("y")
    core = c.astype(jnp.int32)[None]

    all_features = lax.all_gather(features, PLANE, axis=0, tiled=True)
    give = lax.dynamic_slice_in_dim(features, (1 - c) * half, half, 1)
    keep = lax.dynamic_slice_in_dim(features, c * half, half, 1)
    got = swap(give, "c", 1)
    pair = jnp.where(c == 0, jnp.concatenate([keep, got]), jnp.concatenate([got, keep]))
    count = counts.astype(F32)
    count = count + swap(count, "x", 1)

    dpre, rows, share = token_part(counts, pairs, station_weight, upstream, preact, basis)
    count, share, error_late, rows = tie((count, share, error, rows))
    err_give, err_keep = error_part(core, error_late, basis)
    err_got = swap(err_give, "c", 1)
    inv_mean = n_inter / (count + swap(count, "x", 3))

    rows = rows.reshape(2, -1, cols)
    got = swap(mm(pick(rows, 1 - c), weight, ((1,), (1,))).astype(BF16), "c", 1)
    share = lax.all_to_all(share, ("z", "y"), 0, 0, tiled=True).reshape(n_z * n_y, -1, rank)
    grad = (mm(pick(rows, c), weight, ((1,), (1,))) + got.astype(F32)).astype(BF16)
    grad = grad.reshape(n_y, -1, width)
    piece = grad.shape[1] // 2
    far = pick(grad, (y + 2) % n_y)
    far_up, far_down = far[:piece], far[piece:]
    inv_mean, share, err_got, pair, grad, far_up, far_down = tie(
        (inv_mean, share, err_got, pair, grad, far_up, far_down)
    )
    share = share.sum(0)
    part = left_part(inv_mean, share, swap(share, "c", 1), pair, err_keep, err_got)

    up, down = shift(far_up, "y", 1), shift(far_down, "y", -1)
    grad, part = tie((grad, part))
    after, before = pick(grad, (y + 1) % n_y), pick(grad, (y + 3) % n_y)
    after = jnp.concatenate([after[:piece] + up, after[piece:]])
    before = jnp.concatenate([before[:piece], before[piece:] + down])
    part = lax.all_to_all(part, ("x", "y"), 0, 0, tiled=True)
    after, before, part = tie((after, before, part))

    up, down = shift(after, "y", 1), shift(before, "y", -1)
    part = part.reshape(n_inter * n_y, -1, rank).sum(0)
    for bit in (1, 2, 7):
        part = part + swap(part, "z", bit)
    up, down, part = tie((up, down, part))

    mine = lax.all_to_all(
        jnp.broadcast_to(part[None], (n_inter * n_y,) + part.shape), ("x", "y"), 0, 0, tiled=True
    ).reshape(half, rank)
    merged, head, rest = merge_part(inv_mean, all_features, dpre, error)
    grad = pick(grad, y).astype(F32) + up.astype(F32) + down.astype(F32)
    grad = grad.astype(BF16)
    grad, merged, mine = tie((grad, merged, mine))

    other = swap(mine, "c", 1)
    grad = lax.all_to_all(grad, "z", 0, 0, tiled=True)
    right = right_part(core, head, rest, mine, other)
    right_got = swap(right, "x", 1)
    right, mine = tie((right, mine))
    gram = jnp.dot(mine.T, mine, precision=HIGHEST)
    gram = gram + swap(gram, "c", 1)
    gram, right = tie((gram, right + right_got))
    right_got = swap(right, "x", 3)
    inverse = inverse_part(gram)
    new_error, new_basis, grad = last_part(
        core, merged, mine, other, right, right_got, inverse, grad
    )
    return grad, new_error, new_basis


def solution(mesh):
    mesh = Mesh(mesh.devices.reshape(4, 8, 4, 2), ALL)
    in_specs = (
        P(ALL, None),
        P("x", PLANE),
        P("x", PLANE),
        P(None, PLANE),
        P("x", None),
        P(),
        P("x"),
        P("x", PLANE),
        P(PLANE, None),
    )
    out_specs = (P(ALL, None), P("x", PLANE), P(PLANE, None))
    return jax.shard_map(
        per_device, mesh=mesh, in_specs=in_specs, out_specs=out_specs, check_vma=False
    )
```

```python
import functools, math
import jax
import jax.numpy as jnp
from jax import lax
from jax.experimental import pallas as pl
from jax.experimental.pallas import tpu as pltpu
from jax.sharding import Mesh, PartitionSpec as P

F32 = jnp.float32
BF16 = jnp.bfloat16
HIGHEST = lax.Precision.HIGHEST
VMEM = 56 * 1024 * 1024


def gelu_slope(value):
    cdf = 0.5 * (1.0 + lax.erf(value / math.sqrt(2.0)))
    return cdf + value * jnp.exp(-0.5 * value * value) / math.sqrt(2.0 * math.pi)


def split(value):
    head = value.astype(BF16)
    return head, (value - head.astype(F32)).astype(BF16)


def mm(a, b, contract):
    return lax.dot_general(a, b, (contract, ((), ())), preferred_element_type=F32)


def mm_wide(a, wide, contract):
    head, rest = split(wide)
    out = mm(a, jnp.concatenate([head, rest], axis=1), contract)
    n = wide.shape[1]
    return out[:, :n] + out[:, n:]


def mm_split(a, b, contract):
    return mm(a[0], b[0], contract) + (mm(a[0], b[1], contract) + mm(a[1], b[0], contract))


def params(limit=VMEM):
    return pltpu.CompilerParams(vmem_limit_bytes=limit)


def token_kernel(count_ref, pairs_ref, table_ref, up_ref, pre_ref, basis_ref, dpre_ref, rows_ref, share_ref):
    rows = up_ref.shape[0]
    stations = table_ref.shape[1]
    table = table_ref[...]
    head = table.astype(BF16)
    middle = (table - head.astype(F32)).astype(BF16)
    last = (table - head.astype(F32) - middle.astype(F32)).astype(BF16)
    which = lax.broadcasted_iota(jnp.int32, (stations, rows), 0)
    weight = None
    for end in range(2):
        onehot = (which == pairs_ref[end : end + 1, :]).astype(F32).astype(BF16)
        found = None
        for piece in (last, middle, head):
            term = mm(jnp.broadcast_to(piece, (16, stations)), onehot, ((1,), (0,)))[:1]
            found = term if found is None else found + term
        weight = found if weight is None else weight * found
    live = lax.broadcasted_iota(jnp.int32, (1, rows), 1) < count_ref[0]
    weight = jnp.where(live, weight, 0.0)
    column = jnp.transpose(jnp.broadcast_to(weight, (128, rows)))
    column = jnp.concatenate([column] * (up_ref.shape[1] // 128), axis=1)
    wide = up_ref[...].astype(F32) * gelu_slope(pre_ref[...].astype(F32)) * column
    dpre = wide.astype(BF16)
    dpre_ref[...] = dpre
    starts = [
        ((z * 4 + y) * 2 + core) * 8 for core in range(2) for y in range(4) for z in range(rows // 64)
    ]
    rows_ref[...] = jnp.concatenate([wide[s : s + 8] for s in starts], axis=0).astype(BF16)
    share_ref[...] = mm_wide(dpre, basis_ref[...], ((1,), (0,)))


def token_part(counts, pairs, table, upstream, preact, basis):
    vm = pl.BlockSpec(memory_space=pltpu.VMEM)
    return pl.pallas_call(
        token_kernel,
        out_shape=(
            jax.ShapeDtypeStruct(upstream.shape, BF16),
            jax.ShapeDtypeStruct(upstream.shape, BF16),
            jax.ShapeDtypeStruct((upstream.shape[0], basis.shape[1]), F32),
        ),
        in_specs=[pl.BlockSpec(memory_space=pltpu.SMEM)] + [vm] * 5,
        out_specs=(vm, vm, vm),
        compiler_params=params(),
        cost_estimate=pl.CostEstimate(flops=10**5, bytes_accessed=10**4, transcendentals=0),
    )(counts, pairs.T, table[None], upstream, preact, basis)


def err_kernel(core_ref, error_ref, basis_ref, give_ref, keep_ref):
    product = mm_wide(error_ref[...], basis_ref[...], ((1,), (0,)))

    @pl.when(pl.program_id(0) == 0)
    def _():
        give_ref[...] = product

    @pl.when(pl.program_id(0) == 1)
    def _():
        keep_ref[...] = product


def error_part(core, error, basis):
    rows, cols = error.shape
    rank, half = basis.shape[1], rows // 2
    whole = lambda h, core: (0, 0)
    return pl.pallas_call(
        err_kernel,
        out_shape=(jax.ShapeDtypeStruct((half, rank), F32),) * 2,
        grid_spec=pltpu.PrefetchScalarGridSpec(
            num_scalar_prefetch=1,
            grid=(2,),
            in_specs=[
                pl.BlockSpec((half, cols), lambda h, core: ((core[0] + 1 + h) % 2, 0)),
                pl.BlockSpec((cols, rank), whole),
            ],
            out_specs=(pl.BlockSpec((half, rank), whole),) * 2,
        ),
        compiler_params=params(),
        cost_estimate=pl.CostEstimate(flops=10**5, bytes_accessed=10**4, transcendentals=0),
    )(core, error, basis)


def left_kernel(inv_ref, share_ref, other_ref, feat_ref, keep_ref, got_ref, out_ref):
    share = share_ref[...] + other_ref[...]
    out_ref[...] = (
        keep_ref[...]
        + got_ref[...]
        + mm_wide(feat_ref[...], share * inv_ref[0], ((0,), (0,)))
    )


def left_part(inv_mean, share, share_got, feats, keep, got):
    tokens, rank = share.shape
    half = got.shape[0]
    step = half
    rows = pl.BlockSpec((step, rank), lambda i: (i, 0))
    return pl.pallas_call(
        left_kernel,
        out_shape=jax.ShapeDtypeStruct((half, rank), F32),
        grid=(half // step,),
        in_specs=[
            pl.BlockSpec(memory_space=pltpu.SMEM),
            pl.BlockSpec((tokens, rank), lambda i: (0, 0)),
            pl.BlockSpec((tokens, rank), lambda i: (0, 0)),
            pl.BlockSpec((tokens, step), lambda i: (0, i)),
            rows,
            rows,
        ],
        out_specs=rows,
        compiler_params=params(VMEM // 4),
        cost_estimate=pl.CostEstimate(flops=10**8, bytes_accessed=4 * 10**6, transcendentals=0),
    )(inv_mean, share, share_got, feats, keep, got)


def merge_kernel(inv_ref, feat_ref, dpre_ref, error_ref, merged_ref, head_ref, rest_ref):
    raw = mm(feat_ref[...], dpre_ref[...], ((0,), (0,)))
    merged = raw * inv_ref[0] + error_ref[...].astype(F32)
    merged_ref[...] = merged
    head, rest = split(jnp.transpose(merged))
    head_ref[...] = head
    rest_ref[...] = rest


def merge_part(inv_mean, features, dpre, error):
    tokens, width = features.shape
    cols = dpre.shape[1]
    step = 2048
    return pl.pallas_call(
        merge_kernel,
        out_shape=(
            jax.ShapeDtypeStruct((width, cols), F32),
            jax.ShapeDtypeStruct((cols, width), BF16),
            jax.ShapeDtypeStruct((cols, width), BF16),
        ),
        grid=(width // step,),
        in_specs=[
            pl.BlockSpec(memory_space=pltpu.SMEM),
            pl.BlockSpec((tokens, step), lambda i: (0, i)),
            pl.BlockSpec((tokens, cols), lambda i: (0, 0)),
            pl.BlockSpec((step, cols), lambda i: (i, 0)),
        ],
        out_specs=(
            pl.BlockSpec((step, cols), lambda i: (i, 0)),
            pl.BlockSpec((cols, step), lambda i: (0, i)),
            pl.BlockSpec((cols, step), lambda i: (0, i)),
        ),
        compiler_params=params(),
        cost_estimate=pl.CostEstimate(flops=2 * 10**9, bytes_accessed=16 * 10**6, transcendentals=0),
    )(inv_mean, features, dpre, error)


def right_kernel(core_ref, head_ref, rest_ref, own_ref, other_ref, right_ref):
    def term(left):
        lh, ll = split(left)
        rank = lh.shape[1]
        both = mm(head_ref[...], jnp.concatenate([lh, ll], axis=1), ((1,), (0,)))
        return both[:, :rank] + both[:, rank:] + mm(rest_ref[...], lh, ((1,), (0,)))

    @pl.when(pl.program_id(0) == 0)
    def _():
        right_ref[...] = term(own_ref[...])

    @pl.when(pl.program_id(0) == 1)
    def _():
        right_ref[...] += term(other_ref[...])


def right_part(core, head, rest, own, other):
    cols, width = head.shape
    half, rank = own.shape
    whole = lambda h, core: (0, 0)
    column = pl.BlockSpec((cols, half), lambda h, core: (0, (core[0] + h) % 2))
    return pl.pallas_call(
        right_kernel,
        out_shape=jax.ShapeDtypeStruct((cols, rank), F32),
        grid_spec=pltpu.PrefetchScalarGridSpec(
            num_scalar_prefetch=1,
            grid=(2,),
            in_specs=[column, column] + [pl.BlockSpec((half, rank), whole)] * 2,
            out_specs=pl.BlockSpec((cols, rank), whole),
        ),
        compiler_params=params(),
        cost_estimate=pl.CostEstimate(flops=10**9, bytes_accessed=6 * 10**6, transcendentals=0),
    )(core, head, rest, own, other)


def inverse_kernel(gram_ref, out_ref):
    n = gram_ref.shape[0]
    a = gram_ref[...]
    b = (
        lax.broadcasted_iota(jnp.int32, (n, n), 0) == lax.broadcasted_iota(jnp.int32, (n, n), 1)
    ).astype(F32)
    for low in range(0, n, 8):
        left = n - low
        row_index = lax.broadcasted_iota(jnp.int32, (left, n), 0)
        columns = [
            jnp.broadcast_to(a[:, low + j : low + j + 1], (left, n)) for j in range(8)
        ]
        for j in range(8):
            column = columns[j]
            pivot = column[j : j + 1, :]
            scale = lax.rsqrt(pivot)
            scale = scale * (1.5 - 0.5 * pivot * scale * scale)
            row_a, row_b = a[j : j + 1, :], b[j : j + 1, :]
            out_ref[low + j : low + j + 1, :] = row_b * scale
            factor = jnp.where(row_index > j, column * (scale * scale), 0.0)
            for i in range(j + 1, 8):
                columns[i] = columns[i] - factor * column[i : i + 1, :]
            a = a - factor * row_a
            b = b - factor * row_b
        a, b = a[8:], b[8:]


def inverse_part(gram):
    vm = pl.BlockSpec(memory_space=pltpu.VMEM)
    return pl.pallas_call(
        inverse_kernel,
        out_shape=jax.ShapeDtypeStruct(gram.shape, F32),
        in_specs=[vm],
        out_specs=vm,
        compiler_params=params(VMEM // 8),
        cost_estimate=pl.CostEstimate(flops=10**7, bytes_accessed=10**5, transcendentals=128),
    )(gram)


def last_kernel(core_ref, merged_ref, own_ref, other_ref, right_ref, got_ref, inverse_ref, grad_ref, error_ref, basis_ref, sum_ref, back_ref):
    def fill(left):
        lh, ll = split(left)
        head = jnp.concatenate([back_ref[0], back_ref[0]], axis=1)
        out = mm(jnp.concatenate([lh, ll], axis=1), head, ((1,), (1,))) + mm(lh, back_ref[1], ((1,), (1,)))
        error_ref[...] = (merged_ref[...] - out).astype(BF16)

    @pl.when(pl.program_id(0) == 0)
    def _():
        inverse = split(inverse_ref[...])
        basis = mm_split(split(right_ref[...] + got_ref[...]), inverse, ((1,), (1,)))
        basis_ref[...] = basis
        head, rest = split(mm_split(split(basis * 0.25), inverse, ((1,), (0,))))
        back_ref[0] = head
        back_ref[1] = rest
        fill(own_ref[...])
        rows, step = sum_ref.shape[0], 512
        for start in range(0, sum_ref.shape[1], step):
            blocks = grad_ref[:, start : start + step].astype(F32)
            total = blocks[:rows]
            for first in range(rows, blocks.shape[0], rows):
                total = total + blocks[first : first + rows]
            sum_ref[:, start : start + step] = total.astype(BF16)

    pl.when(pl.program_id(0) == 1)(lambda: fill(other_ref[...]))


def last_part(core, merged, own, other, right, got, inverse, grad):
    width, cols = merged.shape
    half, rank = own.shape
    whole = lambda h, core: (0, 0)
    row = pl.BlockSpec((half, cols), lambda h, core: ((core[0] + h) % 2, 0))
    return pl.pallas_call(
        last_kernel,
        out_shape=(
            jax.ShapeDtypeStruct((width, cols), BF16),
            jax.ShapeDtypeStruct((cols, rank), F32),
            jax.ShapeDtypeStruct((8, grad.shape[1]), BF16),
        ),
        grid_spec=pltpu.PrefetchScalarGridSpec(
            num_scalar_prefetch=1,
            grid=(2,),
            in_specs=[
                row,
                pl.BlockSpec((half, rank), whole),
                pl.BlockSpec((half, rank), whole),
                pl.BlockSpec((cols, rank), whole),
                pl.BlockSpec((cols, rank), whole),
                pl.BlockSpec((rank, rank), whole),
                pl.BlockSpec(grad.shape, whole),
            ],
            out_specs=(
                row,
                pl.BlockSpec((cols, rank), whole),
                pl.BlockSpec((8, grad.shape[1]), whole),
            ),
            scratch_shapes=[pltpu.VMEM((2, cols, rank), BF16)],
        ),
        compiler_params=params(),
        cost_estimate=pl.CostEstimate(flops=10**9, bytes_accessed=8 * 10**6, transcendentals=0),
    )(core, merged, own, other, right, got, inverse, grad)


PLANE = ("z", "y", "c")
ALL = ("x", "z", "y", "c")


def swap(value, axis, bit):
    n = lax.axis_size(axis)
    return lax.ppermute(value, axis, [(i, i ^ bit) for i in range(n)])


def shift(value, axis, by):
    n = lax.axis_size(axis)
    return lax.ppermute(value, axis, [(i, (i + by) % n) for i in range(n)])


def pick(value, index):
    return lax.dynamic_index_in_dim(value, index, 0, keepdims=False)


def per_device(features, preact, upstream, weight, pairs, station_weight, counts, error, basis):
    tie = lax.optimization_barrier
    n_inter, n_z, n_y = lax.axis_size("x"), lax.axis_size("z"), lax.axis_size("y")
    group_rows, width = preact.shape[0], features.shape[1]
    rank, half = basis.shape[1], width // 2
    cols = preact.shape[1]
    c, y = lax.axis_index("c"), lax.axis_index("y")
    core = c.astype(jnp.int32)[None]

    all_features = lax.all_gather(features, PLANE, axis=0, tiled=True)
    give = lax.dynamic_slice_in_dim(features, (1 - c) * half, half, 1)
    keep = lax.dynamic_slice_in_dim(features, c * half, half, 1)
    got = swap(give, "c", 1)
    pair = jnp.where(c == 0, jnp.concatenate([keep, got]), jnp.concatenate([got, keep]))
    count = counts.astype(F32)
    count = count + swap(count, "x", 1)

    dpre, rows, share = token_part(counts, pairs, station_weight, upstream, preact, basis)
    count, share, error_late, rows = tie((count, share, error, rows))
    err_give, err_keep = error_part(core, error_late, basis)
    err_got = swap(err_give, "c", 1)
    inv_mean = n_inter / (count + swap(count, "x", 3))

    rows = rows.reshape(2, -1, cols)
    got = swap(mm(pick(rows, 1 - c), weight, ((1,), (1,))).astype(BF16), "c", 1)
    share = lax.all_to_all(share, ("z", "y"), 0, 0, tiled=True).reshape(n_z * n_y, -1, rank)
    grad = (mm(pick(rows, c), weight, ((1,), (1,))) + got.astype(F32)).astype(BF16)
    grad = grad.reshape(n_y, -1, width)
    piece = grad.shape[1] // 2
    far = pick(grad, (y + 2) % n_y)
    far_up, far_down = far[:piece], far[piece:]
    inv_mean, share, err_got, pair, grad, far_up, far_down = tie(
        (inv_mean, share, err_got, pair, grad, far_up, far_down)
    )
    share = share.sum(0)
    part = left_part(inv_mean, share, swap(share, "c", 1), pair, err_keep, err_got)

    up, down = shift(far_up, "y", 1), shift(far_down, "y", -1)
    grad, part = tie((grad, part))
    after, before = pick(grad, (y + 1) % n_y), pick(grad, (y + 3) % n_y)
    after = jnp.concatenate([after[:piece] + up, after[piece:]])
    before = jnp.concatenate([before[:piece], before[piece:] + down])
    part = lax.all_to_all(part, ("x", "y"), 0, 0, tiled=True)
    after, before, part = tie((after, before, part))

    up, down = shift(after, "y", 1), shift(before, "y", -1)
    part = part.reshape(n_inter * n_y, -1, rank).sum(0)
    for bit in (1, 2, 7):
        part = part + swap(part, "z", bit)
    up, down, part = tie((up, down, part))

    mine = lax.all_to_all(
        jnp.broadcast_to(part[None], (n_inter * n_y,) + part.shape), ("x", "y"), 0, 0, tiled=True
    ).reshape(half, rank)
    merged, head, rest = merge_part(inv_mean, all_features, dpre, error)
    grad = pick(grad, y).astype(F32) + up.astype(F32) + down.astype(F32)
    grad = grad.astype(BF16)
    grad, merged, mine = tie((grad, merged, mine))

    other = swap(mine, "c", 1)
    grad = lax.all_to_all(grad, "z", 0, 0, tiled=True)
    right = right_part(core, head, rest, mine, other)
    right_got = swap(right, "x", 1)
    right, mine = tie((right, mine))
    gram = jnp.dot(mine.T, mine, precision=HIGHEST)
    gram = gram + swap(gram, "c", 1)
    gram, right = tie((gram, right + right_got))
    right_got = swap(right, "x", 3)
    inverse = inverse_part(gram)
    new_error, new_basis, grad = last_part(
        core, merged, mine, other, right, right_got, inverse, grad
    )
    return grad, new_error, new_basis


def solution(mesh):
    mesh = Mesh(mesh.devices.reshape(4, 8, 4, 2), ALL)
    in_specs = (
        P(ALL, None),
        P("x", PLANE),
        P("x", PLANE),
        P(None, PLANE),
        P("x", None),
        P(),
        P("x"),
        P("x", PLANE),
        P(PLANE, None),
    )
    out_specs = (P(ALL, None), P("x", PLANE), P(PLANE, None))
    return jax.shard_map(
        per_device, mesh=mesh, in_specs=in_specs, out_specs=out_specs, check_vma=False
    )
```
